32 devices in a mesh: dp: 2 (over y), cell: 4 (over z), gene: 4 (over x, core).
Axes of the slice: x: 2, y: 2, z: 4, core: 2. Of those that a mesh axis runs over, the one named last changes fastest.
Arguments:
- expression: bfloat16 [4000, 8192], P('gene', ('dp', 'cell')), may hold values from 0.15 to 40
- usage_init: float32 [64, 8192], P(None, ('dp', 'cell')), may hold values from 0.1 to 1.5
- shared_factor: float32 [64, 4000], P(None, 'gene'), may hold values from 0.03 to 1
- dataset_factors: float32 [10, 64, 4000], P('dp', None, 'gene'), may hold values from 0.03 to 1
- cell_dataset: int32 [8192], P(('dp', 'cell')), may hold values from 0 to 5, as said below
- dataset_sizes: int32 [10], P('dp'), may hold values from 1 to 4092, as said below
Outputs:
- new_usage: float32 [64, 8192], P(None, ('dp', 'cell'))
- new_dataset_factors: float32 [10, 64, 4000], P('dp', None, 'gene')
- new_shared_factor: float32 [64, 4000], P(None, 'gene')
The draws below stay inside these ranges and needn't reach their ends.
Inputs may be any that keep to these rules, and one draw needn't show every extreme that they name: `cell_dataset`: each group's live slots come first, a value of 5 marks an empty slot, every dataset has at least one live slot in every group, and one group has all its 4096 slots live. `dataset_sizes`: the number of live slots of each dataset within its group, as counted from cell_dataset; some dataset has exactly 4092 of them.
All inputs are finite; a program needn't handle non-finite values.
Results may differ from the reference program's by a relative error of at most 0.0003.
The reference program's roundings to bfloat16 on the way count: a program that leaves them out, or rounds other values in their place, can miss the bound.
Values sent between devices are 32-bit elements; how exact they have to be, the bound alone decides.
No kernel may reach another device: no remote copies, remote signals or barrier semaphores. Data moves between devices by JAX's collectives and lax.ppermute only.
A program may use at most 64 MiB of HBM per device.

```python
import math
import jax
import jax.numpy as jnp
from jax import lax

GENES = 4000
K = 64
DSETS = 5
ITERS = 3
GROUPS = 2
SLOTS = 4096
CELLS = 8192
DATASETS = 10


def labels_and_sizes(key):
    base = jax.random.fold_in(key, 7101)
    full_group = jax.random.randint(jax.random.fold_in(base, 1), (), 0, GROUPS)
    leading = jax.random.randint(jax.random.fold_in(base, 4), (), 0, DSETS)
    partial_counts = jax.random.randint(jax.random.fold_in(base, 2), (GROUPS,), SLOTS // 8, SLOTS // 3 + 1)
    is_full = jnp.arange(GROUPS) == full_group
    live_counts = jnp.where(is_full, SLOTS, partial_counts)
    position = jnp.arange(SLOTS)[None, :]
    picked = jax.random.randint(jax.random.fold_in(base, 3), (GROUPS, SLOTS), 0, DSETS)
    picked = jnp.where(is_full[:, None], leading, picked)
    picked = jnp.where(position < DSETS, position, picked)
    labels = jnp.where(position < live_counts[:, None], picked, DSETS).astype(jnp.int32)
    counted = jnp.sum((labels[:, :, None] == jnp.arange(DSETS)[None, None, :]).astype(jnp.int32), axis=1)
    return (labels.reshape(CELLS), counted.reshape(DATASETS).astype(jnp.int32))


def draw_cell_dataset(key, part):
    return labels_and_sizes(key)[0]


def draw_dataset_sizes(key, part):
    return labels_and_sizes(key)[1]


def draw_expression(key, part):
    base = jax.random.fold_in(key, 3301)
    entry = jnp.exp(jax.random.uniform(jax.random.fold_in(base, 1), (GENES, CELLS), jnp.float32, math.log(0.7), math.log(6.5)))
    slot = (jnp.arange(CELLS) % SLOTS).astype(jnp.float32)
    trend = -0.6 + 1.5 * slot / SLOTS
    rough = jax.random.uniform(jax.random.fold_in(base, 2), (CELLS,), jnp.float32, -0.9, 0.9)
    level = jnp.exp(trend + rough)
    return (entry * level[None, :]).astype(jnp.bfloat16)


def gene_levels(key):
    return jnp.exp(jax.random.uniform(jax.random.fold_in(key, 8821), (GENES,), jnp.float32, -1.0, 1.0))


def factor_entries(key, shape):
    entry = jnp.exp(jax.random.uniform(key, shape, jnp.float32, math.log(0.1), math.log(0.36)))
    return entry


def draw_shared_factor(key, part):
    entry = factor_entries(jax.random.fold_in(key, 4411), (K, GENES))
    return (entry * gene_levels(key)[None, :]).astype(jnp.float32)


def draw_dataset_factors(key, part):
    entry = factor_entries(jax.random.fold_in(key, 4477), (DATASETS, K, GENES))
    return (entry * gene_levels(key)[None, None, :]).astype(jnp.float32)


def level_of(own_key, extent, split, smallest, high):
    def one(dim, blocks):
        steps = jax.random.uniform(jax.random.fold_in(jax.random.fold_in(own_key, 6), dim), (blocks,), jnp.float32, smallest / len(split), high / len(split))
        return jnp.repeat(jnp.exp(steps), extent[dim] // blocks).reshape((-1,) + (1,) * (len(extent) - dim - 1))

    level = one(*split[0])
    for cut in split[1:]:
        level = level * one(*cut)
    return level


def setup_inputs(seed: int = 0) -> dict:
    splits = jax.random.split(jax.random.key(seed), 7)
    return {
        "expression": draw_expression(jax.random.fold_in(splits[6], 71), 0),
        "usage_init": jnp.clip(jnp.exp(math.log(1.5) - 2.7080502 * jax.random.uniform(splits[1], (K, CELLS), jnp.float32) ** level_of(splits[1], (K, CELLS), ((1, 8),), -0.2, 0.2)), 0.1, 1.5),
        "shared_factor": draw_shared_factor(jax.random.fold_in(splits[6], 71), 0),
        "dataset_factors": draw_dataset_factors(jax.random.fold_in(splits[6], 71), 0),
        "cell_dataset": draw_cell_dataset(jax.random.fold_in(splits[6], 71), 0),
        "dataset_sizes": draw_dataset_sizes(jax.random.fold_in(splits[6], 71), 0),
    }


penalty = 5.0
precise = lax.Precision.HIGHEST


def reference(expression, usage_init, shared_factor, dataset_factors, cell_dataset, dataset_sizes):
    shared_low = shared_factor.astype(jnp.bfloat16)
    usage_blocks = []
    cross_blocks = []
    gram_blocks = []
    for group in range(GROUPS):
        first_cell = group * SLOTS
        block_expr = expression[:, first_cell:first_cell + SLOTS]
        labels = cell_dataset[first_cell:first_cell + SLOTS]
        factors = dataset_factors[group * DSETS:(group + 1) * DSETS]
        counted = dataset_sizes[group * DSETS:(group + 1) * DSETS].astype(jnp.float32)
        onehot = (labels[None, :] == jnp.arange(DSETS, dtype=jnp.int32)[:, None]).astype(jnp.float32)
        alive_mask = labels < DSETS
        shared_term = jnp.dot(shared_low, block_expr, preferred_element_type=jnp.float32)
        own_terms = jnp.dot(factors.astype(jnp.bfloat16).reshape(DSETS * K, GENES), block_expr,
                            preferred_element_type=jnp.float32).reshape(DSETS, K, SLOTS)
        cross_sum = shared_term + jnp.sum(onehot[:, None, :] * own_terms, axis=0)
        combined = shared_factor[None] + factors
        gram_full = jnp.einsum("dkg,dlg->dkl", combined, combined, precision=precise) + penalty * jnp.einsum(
            "dkg,dlg->dkl", factors, factors, precision=precise)
        usage_now = usage_init[:, first_cell:first_cell + SLOTS]
        for sweep in range(ITERS):
            stacked = jnp.einsum("dkl,lc->dkc", gram_full, usage_now, precision=precise)
            divisor = jnp.sum(onehot[:, None, :] * stacked, axis=0)
            divisor = jnp.where(alive_mask[None, :], divisor, 1.0)
            usage_now = jnp.where(alive_mask[None, :], usage_now * cross_sum / divisor, usage_now)
        usage_blocks.append(usage_now)
        masked_usage = onehot[:, None, :] * usage_now[None]
        low_usage = masked_usage.astype(jnp.bfloat16).reshape(DSETS * K, SLOTS)
        stat_cross = lax.dot_general(low_usage, block_expr, (((1,), (1,)), ((), ())),
                                     preferred_element_type=jnp.float32).reshape(DSETS, K, GENES)
        cross_blocks.append(stat_cross / counted[:, None, None])
        stat_gram = jnp.einsum("dkc,dlc->dkl", masked_usage, masked_usage, precision=precise)
        gram_blocks.append(stat_gram / counted[:, None, None])
    stat_cross = jnp.concatenate(cross_blocks, axis=0)
    stat_gram = jnp.concatenate(gram_blocks, axis=0)
    factor_now = dataset_factors
    for sweep in range(ITERS):
        divisor = jnp.einsum("dkl,lg->dkg", stat_gram, shared_factor, precision=precise) + (1.0 + penalty) * jnp.einsum(
            "dkl,dlg->dkg", stat_gram, factor_now, precision=precise)
        factor_now = factor_now * stat_cross / divisor
    total_cross = jnp.sum(stat_cross, axis=0)
    total_gram = jnp.sum(stat_gram, axis=0)
    total_pull = jnp.einsum("dkl,dlg->kg", stat_gram, factor_now, precision=precise)
    shared_now = shared_factor
    for sweep in range(ITERS):
        shared_now = shared_now * total_cross / (jnp.dot(total_gram, shared_now, precision=precise) + total_pull)
    return jnp.concatenate(usage_blocks, axis=1), factor_now, shared_now
```

```python
import functools

import jax
import jax.numpy as jnp
from jax import lax
from jax.experimental import pallas as pl
from jax.experimental.pallas import tpu as pltpu
from jax.sharding import PartitionSpec as P

ITERS = 3
penalty = 5.0
precise = lax.Precision.HIGHEST
f32 = jnp.float32
bf16 = jnp.bfloat16

GENE_TILE = 256
VMEM = pl.BlockSpec(memory_space=pltpu.VMEM)


def shared_update(shared_now, total_cross, total_gram, total_pull):
    for sweep in range(ITERS):
        shared_now = (
            shared_now
            * total_cross
            / (jnp.dot(total_gram, shared_now, precision=precise) + total_pull)
        )
    return shared_now


def plain_body(expression, usage_init, shared_factor, dataset_factors, cell_dataset, dataset_sizes):
    dataset_count = dataset_factors.shape[0]
    factor_rank = shared_factor.shape[0]
    gene_count = shared_factor.shape[1]
    slot_count = expression.shape[1]
    counted = dataset_sizes.astype(f32)
    onehot = (cell_dataset[None, :] == jnp.arange(dataset_count, dtype=jnp.int32)[:, None]).astype(f32)
    alive_mask = cell_dataset < dataset_count
    stacked_low = jnp.concatenate([shared_factor[None], dataset_factors], axis=0).astype(bf16)
    products = jnp.dot(
        stacked_low.reshape((dataset_count + 1) * factor_rank, gene_count),
        expression,
        preferred_element_type=f32,
    ).reshape(dataset_count + 1, factor_rank, slot_count)
    cross_part = products[0] + jnp.sum(onehot[:, None, :] * products[1:], axis=0)
    combined = shared_factor[None] + dataset_factors
    gram_part = jnp.einsum(
        "dkg,dlg->dkl", combined, combined, precision=precise
    ) + penalty * jnp.einsum("dkg,dlg->dkl", dataset_factors, dataset_factors, precision=precise)
    cross_sum, gram_full = lax.psum((cross_part, gram_part), "gene")
    usage_now = usage_init
    for sweep in range(ITERS):
        stacked = jnp.dot(
            gram_full.reshape(dataset_count * factor_rank, factor_rank),
            usage_now,
            precision=precise,
        ).reshape(dataset_count, factor_rank, slot_count)
        divisor = jnp.sum(onehot[:, None, :] * stacked, axis=0)
        divisor = jnp.where(alive_mask[None, :], divisor, 1.0)
        usage_now = jnp.where(alive_mask[None, :], usage_now * cross_sum / divisor, usage_now)
    masked_usage = onehot[:, None, :] * usage_now[None]
    low_usage = masked_usage.astype(bf16).reshape(dataset_count * factor_rank, slot_count)
    cross_stat_part = lax.dot_general(
        low_usage, expression, (((1,), (1,)), ((), ())), preferred_element_type=f32
    ).reshape(dataset_count, factor_rank, gene_count)
    cross_stat_part = cross_stat_part / counted[:, None, None]
    gram_stat_part = (
        jnp.einsum("dkc,dlc->dkl", masked_usage, masked_usage, precision=precise)
        / counted[:, None, None]
    )
    stat_cross, stat_gram = lax.psum((cross_stat_part, gram_stat_part), "cell")
    total_cross = jnp.sum(stat_cross, axis=0)
    total_gram = jnp.sum(stat_gram, axis=0)
    factor_now = dataset_factors
    for sweep in range(ITERS):
        divisor = jnp.einsum("dkl,lg->dkg", stat_gram, shared_factor, precision=precise) + (
            1.0 + penalty
        ) * jnp.einsum("dkl,dlg->dkg", stat_gram, factor_now, precision=precise)
        factor_now = factor_now * stat_cross / divisor
    total_pull = jnp.einsum("dkl,dlg->kg", stat_gram, factor_now, precision=precise)
    total_cross, total_gram, total_pull = lax.psum((total_cross, total_gram, total_pull), "dp")
    shared_now = shared_update(shared_factor, total_cross, total_gram, total_pull)
    return (usage_now, factor_now, shared_now)


def halves(value):
    high = value.astype(bf16)
    low = (value - high.astype(f32)).astype(bf16)
    return high, low


def nt_dot(a, b):
    return lax.dot_general(a, b, (((1,), (1,)), ((), ())), preferred_element_type=f32)


def symmetric_product(high, low):
    rank = high.shape[0]
    both = nt_dot(high, jnp.concatenate([high, low], axis=0))
    mixed = both[:, rank:]
    return both[:, :rank] + mixed + mixed.T


def left_cat(matrix):
    high, low = halves(matrix)
    return jnp.concatenate([high, low, high], axis=1)


def right_cat(value):
    high, low = halves(value)
    return jnp.concatenate([high, high, low], axis=0)


def pack_rows(blocks, groups):
    rows = []
    for b in range(groups):
        other = blocks[b + groups] if b + groups < len(blocks) else jnp.zeros_like(blocks[b])
        rows.append(jnp.concatenate([blocks[b], other], axis=1))
    return jnp.concatenate(rows, axis=0)


def unpack(packed, e, groups, rank):
    row = (e % groups) * rank
    lane = (e // groups) * rank
    return packed[row : row + rank, lane : lane + rank]


def gram_kernel(shared_ref, factors_ref, gram_ref, low_ref):
    count, rank, genes = factors_ref.shape
    shared = shared_ref[...]
    low_ref[:rank, :] = shared.astype(bf16)
    blocks = []
    for e in range(count):
        own = factors_ref[e]
        own_high, own_low = halves(own)
        low_ref[(e + 1) * rank : (e + 2) * rank, :] = own_high
        both_high, both_low = halves(shared + own)
        blocks.append(
            symmetric_product(both_high, both_low) + penalty * symmetric_product(own_high, own_low)
        )
    gram_ref[...] = pack_rows(blocks, (count + 1) // 2)


def cross_kernel(index_ref, low_ref, expression_ref, label_ref, send_ref, keep_ref):
    step = pl.program_id(0)
    rank = send_ref.shape[0]
    count = low_ref.shape[0] // rank - 1
    width = expression_ref.shape[1]
    products = jnp.dot(low_ref[...], expression_ref[...], preferred_element_type=f32)
    label = label_ref[...]
    total = products[:rank]
    for e in range(count):
        total += jnp.where(label == e, products[(e + 1) * rank : (e + 2) * rank], 0.0)
    tiles = send_ref.shape[1] // width
    for t in range(tiles):
        @pl.when(step == t)
        def _():
            send_ref[:, t * width : (t + 1) * width] = total

        @pl.when(step == tiles + t)
        def _():
            keep_ref[:, t * width : (t + 1) * width] = total


def usage_kernel(index_ref, own_ref, other_ref, gram_ref, more_ref, usage_ref, label_ref, out_ref):
    rank = usage_ref.shape[0]
    groups = gram_ref.shape[0] // rank
    count = 2 * groups - 1
    gram = gram_ref[...] + more_ref[...]
    left = left_cat(jnp.concatenate([unpack(gram, e, groups, rank) for e in range(count)], axis=0))
    cross = own_ref[...] + other_ref[...]
    label = label_ref[...]
    alive = label < count
    usage = usage_ref[...]
    for sweep in range(ITERS):
        stacked = jnp.dot(left, right_cat(usage), preferred_element_type=f32)
        divisor = jnp.where(alive, 0.0, 1.0)
        for e in range(count):
            divisor += jnp.where(label == e, stacked[e * rank : (e + 1) * rank], 0.0)
        usage = jnp.where(alive, usage * cross / divisor, usage)
    out_ref[...] = usage


def stat_kernel(
    index_ref, own_ref, other_ref, label_ref, expression_ref,
    usage_ref, gram_ref, own_out, out1, out2, out3, low_ref,
):
    step = pl.program_id(0)
    rank, half = own_ref.shape
    count = low_ref.shape[0] // rank
    groups = (count + 1) // 2

    @pl.when(step == 0)
    def _():
        core = index_ref[0]
        usage_ref[:, pl.ds(pl.multiple_of(core * half, half), half)] = own_ref[...]
        usage_ref[:, pl.ds(pl.multiple_of((1 - core) * half, half), half)] = other_ref[...]
        usage = usage_ref[...]
        label = label_ref[...]
        high, low = halves(usage)
        right = jnp.concatenate([high, low], axis=0)
        blocks = []
        for e in range(count):
            mask = label == e
            masked = jnp.where(mask, high, jnp.zeros_like(high))
            low_ref[e * rank : (e + 1) * rank, :] = masked
            both = nt_dot(masked, right)
            mixed = both[:, rank:]
            blocks.append(both[:, :rank] + mixed + mixed.T)
        gram_ref[...] = pack_rows(blocks, groups)

    result = nt_dot(low_ref[...], expression_ref[...])
    for t, ref in enumerate((out3, out2, out1, own_out)):
        @pl.when(step == t)
        def _():
            ref[...] = result


def factor_kernel(
    index_ref, size_ref, cross0, cross1, cross2, cross3, gram_ref, shared_ref, factors_ref,
    out_ref, total_ref,
):
    count, rank, width = factors_ref.shape
    groups = (count + 1) // 2
    gram = gram_ref[...]
    shared = shared_ref[...]
    total_cross = jnp.zeros((rank, width), f32)
    total_pull = jnp.zeros((rank, width), f32)
    for e in range(count):
        rows = slice(e * rank, (e + 1) * rank)
        cross = (cross0[rows, :] + cross1[rows, :]) + (cross2[rows, :] + cross3[rows, :])
        cross = cross / size_ref[e].astype(f32)
        left = left_cat(unpack(gram, e, groups, rank))
        factor = factors_ref[e]
        for sweep in range(ITERS):
            divisor = jnp.dot(
                left, right_cat(shared + (1.0 + penalty) * factor), preferred_element_type=f32
            )
            factor = factor * cross / divisor
        out_ref[rows, :] = factor
        total_cross += cross
        total_pull += jnp.dot(left, right_cat(factor), preferred_element_type=f32)
    total_ref[:rank, :] = total_cross
    total_ref[rank:, :] = total_pull


def gram_total_kernel(index_ref, size_ref, own_ref, other_ref, gram_ref, total_ref):
    half = own_ref.shape[0]
    rank = total_ref.shape[0]
    groups = gram_ref.shape[0] // rank
    count = 2 * groups - 1
    core = index_ref[0]
    gram_ref[pl.ds(pl.multiple_of(core * half, half), half), :] = own_ref[...]
    gram_ref[pl.ds(pl.multiple_of((1 - core) * half, half), half), :] = other_ref[...]
    total = jnp.zeros((rank, rank), f32)
    for e in range(count):
        row = (e % groups) * rank
        lane = (e // groups) * rank
        scaled = gram_ref[row : row + rank, lane : lane + rank] / size_ref[e].astype(f32)
        gram_ref[row : row + rank, lane : lane + rank] = scaled
        total += scaled
    total_ref[...] = jnp.concatenate([total, jnp.zeros_like(total)], axis=1)


def shared_kernel(index_ref, own_ref, other_ref, gram_own, gram_other, shared_ref, out_ref):
    rank = shared_ref.shape[0]
    total = own_ref[...] + other_ref[...]
    left = left_cat((gram_own[...] + gram_other[...])[:, :rank])
    shared = shared_ref[...]
    for sweep in range(ITERS):
        divisor = jnp.dot(left, right_cat(shared), preferred_element_type=f32) + total[rank:]
        shared = shared * total[:rank] / divisor
    out_ref[...] = shared


def place_kernel(index_ref, f0, f1, f2, f3, s0, s1, s2, s3, factors_ref, shared_ref):
    step = pl.program_id(0)
    count, rank, width = factors_ref.shape
    for t, (f, s) in enumerate(((f0, s0), (f1, s1), (f2, s2), (f3, s3))):
        @pl.when(step == t)
        def _():
            factors_ref[...] = f[...].reshape(count, rank, width)
            shared_ref[...] = s[...]


def struct(*shape, dtype=f32):
    return jax.ShapeDtypeStruct(shape, dtype)


def whole(shape):
    return pl.BlockSpec(shape, lambda *_: (0,) * len(shape))


def call(kernel, index, args, in_specs, out_shape, out_specs, grid=(1,), scratch=(), cost=None):
    return pl.pallas_call(
        kernel,
        grid_spec=pltpu.PrefetchScalarGridSpec(
            num_scalar_prefetch=len(index),
            grid=grid,
            in_specs=in_specs,
            out_specs=out_specs,
            scratch_shapes=list(scratch),
        ),
        out_shape=out_shape,
        compiler_params=pltpu.CompilerParams(vmem_limit_bytes=32 * 1024 * 1024),
        cost_estimate=cost,
    )(*index, *args)


def cost(flops, moved):
    return pl.CostEstimate(flops=int(flops), bytes_accessed=int(moved), transcendentals=0)


def fast_body(expression, usage_init, shared_factor, dataset_factors, cell_dataset, dataset_sizes):
    count, rank, genes = dataset_factors.shape
    cells = expression.shape[1]
    half = cells // 2
    tile = GENE_TILE
    groups = (count + 1) // 2
    core = lax.axis_index("gene") % 2
    depth = lax.axis_index("cell")
    index = jnp.stack([core, depth]).astype(jnp.int32)
    label = cell_dataset.reshape(1, cells)

    def swap(value, axis, offset, size):
        return lax.ppermute(value, axis, [(i, i ^ offset) for i in range(size)])

    gram_part, low = pl.pallas_call(
        gram_kernel,
        in_specs=[VMEM, VMEM],
        out_specs=[VMEM, VMEM],
        out_shape=[struct(groups * rank, 2 * rank), struct((count + 1) * rank, genes, dtype=bf16)],
        cost_estimate=cost(4 * 4 * count * rank * rank * genes, 8 * count * rank * genes),
    )(shared_factor, dataset_factors)
    gram_part = gram_part + swap(gram_part, "gene", 2, 4)
    gram_more = swap(gram_part, "gene", 1, 4)

    cell_tile = 256
    tiles = half // cell_tile

    def cell_block(i, idx):
        other = i // tiles == 0
        which = jnp.where(other, 1 - idx[0], idx[0])
        return which * tiles + i % tiles

    send, keep = call(
        cross_kernel,
        (index,),
        (low, expression, label),
        [
            whole(low.shape),
            pl.BlockSpec((genes, cell_tile), lambda i, idx: (0, cell_block(i, idx))),
            pl.BlockSpec((1, cell_tile), lambda i, idx: (0, cell_block(i, idx))),
        ],
        [struct(rank, half), struct(rank, half)],
        [whole((rank, half)), whole((rank, half))],
        grid=(2 * tiles,),
        cost=cost(2 * low.shape[0] * genes * cells, 2 * genes * cells),
    )
    cross = keep + swap(send, "gene", 1, 4)
    cross_more = swap(cross, "gene", 2, 4)

    usage_half = call(
        usage_kernel,
        (index,),
        (cross, cross_more, gram_part, gram_more, usage_init, label),
        [
            whole(cross.shape),
            whole(cross.shape),
            whole(gram_part.shape),
            whole(gram_part.shape),
            pl.BlockSpec((rank, half), lambda i, idx: (0, idx[0])),
            pl.BlockSpec((1, half), lambda i, idx: (0, idx[0])),
        ],
        struct(rank, half),
        whole((rank, half)),
        cost=cost(2 * ITERS * 3 * count * rank * rank * half, 16 * rank * half),
    )
    usage_other = swap(usage_half, "gene", 1, 4)

    rows = count * rank
    usage, stat_gram, part0, part1, part2, part3 = call(
        stat_kernel,
        (index,),
        (usage_half, usage_other, label, expression),
        [
            whole((rank, half)),
            whole((rank, half)),
            whole((1, cells)),
            pl.BlockSpec((tile, cells), lambda i, idx: (idx[1] ^ (3 - i), 0)),
        ],
        [struct(rank, cells), struct(groups * rank, 2 * rank)] + [struct(rows, tile)] * 4,
        [whole((rank, cells)), whole((groups * rank, 2 * rank))] + [whole((rows, tile))] * 4,
        grid=(4,),
        scratch=[pltpu.VMEM((rows, cells), bf16)],
        cost=cost(2 * rows * genes * cells, 2 * genes * cells),
    )

    got3 = swap(part3, "cell", 3, 4)
    got2 = swap(part2, "cell", 2, 4)
    got1 = swap(part1, "cell", 1, 4)
    gram_rows = groups * rank // 2
    gram_half = lax.dynamic_slice_in_dim(stat_gram, core * gram_rows, gram_rows, 0)
    gram_half = gram_half + swap(gram_half, "cell", 1, 4)
    gram_half = gram_half + swap(gram_half, "cell", 2, 4)
    gram_next = swap(gram_half, "gene", 1, 4)
    gram_scaled, gram_total = call(
        gram_total_kernel,
        (index, dataset_sizes),
        (gram_half, gram_next),
        [whole((gram_rows, 2 * rank))] * 2,
        [struct(groups * rank, 2 * rank), struct(rank, 2 * rank)],
        [whole((groups * rank, 2 * rank)), whole((rank, 2 * rank))],
    )
    gram_total_other = swap(gram_total, "dp", 1, 2)

    gene_block = pl.BlockSpec((rank, tile), lambda i, idx, *_: (0, idx[1]))
    own_factor, total = call(
        factor_kernel,
        (index, dataset_sizes),
        (part0, got1, got2, got3, gram_scaled, shared_factor, dataset_factors),
        [whole((rows, tile))] * 4
        + [
            whole((groups * rank, 2 * rank)),
            gene_block,
            pl.BlockSpec((count, rank, tile), lambda i, idx, *_: (0, 0, idx[1])),
        ],
        [struct(rows, tile), struct(2 * rank, tile)],
        [whole((rows, tile)), whole((2 * rank, tile))],
        cost=cost(2 * 4 * 3 * rows * rank * tile, 6 * 4 * rows * tile),
    )
    total_other = swap(total, "dp", 1, 2)
    factors = [own_factor] + [swap(own_factor, "cell", d, 4) for d in (1, 2, 3)]
    own_shared = call(
        shared_kernel,
        (index,),
        (total, total_other, gram_total, gram_total_other, shared_factor),
        [whole((2 * rank, tile))] * 2 + [whole((rank, 2 * rank))] * 2 + [gene_block],
        struct(rank, tile),
        whole((rank, tile)),
        cost=cost(2 * 3 * 3 * rank * rank * tile, 6 * 4 * rank * tile),
    )
    shareds = [own_shared] + [swap(own_shared, "cell", d, 4) for d in (1, 2, 3)]
    new_factors, new_shared = call(
        place_kernel,
        (index,),
        (*factors, *shareds),
        [whole((rows, tile))] * 4 + [whole((rank, tile))] * 4,
        [struct(count, rank, genes), struct(rank, genes)],
        [
            pl.BlockSpec((count, rank, tile), lambda i, idx: (0, 0, idx[1] ^ i)),
            pl.BlockSpec((rank, tile), lambda i, idx: (0, idx[1] ^ i)),
        ],
        grid=(4,),
        cost=cost(0, 8 * rows * genes),
    )
    return usage, new_factors, new_shared


def solution(mesh):
    sizes = (mesh.shape["dp"], mesh.shape["cell"], mesh.shape["gene"])
    return jax.shard_map(
        fast_body if sizes == (2, 4, 4) else plain_body,
        mesh=mesh,
        in_specs=(
            P("gene", ("dp", "cell")),
            P(None, ("dp", "cell")),
            P(None, "gene"),
            P("dp", None, "gene"),
            P(("dp", "cell")),
            P("dp"),
        ),
        out_specs=(P(None, ("dp", "cell")), P("dp", None, "gene"), P(None, "gene")),
        check_vma=False,
    )
```

```python
import functools

import jax
import jax.numpy as jnp
from jax import lax
from jax.experimental import pallas as pl
from jax.experimental.pallas import tpu as pltpu
from jax.sharding import PartitionSpec as P

ITERS = 3
penalty = 5.0
precise = lax.Precision.HIGHEST
f32 = jnp.float32
bf16 = jnp.bfloat16

GENE_TILE = 256
SPARE = 24
VMEM = pl.BlockSpec(memory_space=pltpu.VMEM)


def shared_update(shared_now, total_cross, total_gram, total_pull):
    for sweep in range(ITERS):
        shared_now = (
            shared_now
            * total_cross
            / (jnp.dot(total_gram, shared_now, precision=precise) + total_pull)
        )
    return shared_now


def plain_body(expression, usage_init, shared_factor, dataset_factors, cell_dataset, dataset_sizes):
    dataset_count = dataset_factors.shape[0]
    factor_rank = shared_factor.shape[0]
    gene_count = shared_factor.shape[1]
    slot_count = expression.shape[1]
    counted = dataset_sizes.astype(f32)
    onehot = (cell_dataset[None, :] == jnp.arange(dataset_count, dtype=jnp.int32)[:, None]).astype(f32)
    alive_mask = cell_dataset < dataset_count
    stacked_low = jnp.concatenate([shared_factor[None], dataset_factors], axis=0).astype(bf16)
    products = jnp.dot(
        stacked_low.reshape((dataset_count + 1) * factor_rank, gene_count),
        expression,
        preferred_element_type=f32,
    ).reshape(dataset_count + 1, factor_rank, slot_count)
    cross_part = products[0] + jnp.sum(onehot[:, None, :] * products[1:], axis=0)
    combined = shared_factor[None] + dataset_factors
    gram_part = jnp.einsum(
        "dkg,dlg->dkl", combined, combined, precision=precise
    ) + penalty * jnp.einsum("dkg,dlg->dkl", dataset_factors, dataset_factors, precision=precise)
    cross_sum, gram_full = lax.psum((cross_part, gram_part), "gene")
    usage_now = usage_init
    for sweep in range(ITERS):
        stacked = jnp.dot(
            gram_full.reshape(dataset_count * factor_rank, factor_rank),
            usage_now,
            precision=precise,
        ).reshape(dataset_count, factor_rank, slot_count)
        divisor = jnp.sum(onehot[:, None, :] * stacked, axis=0)
        divisor = jnp.where(alive_mask[None, :], divisor, 1.0)
        usage_now = jnp.where(alive_mask[None, :], usage_now * cross_sum / divisor, usage_now)
    masked_usage = onehot[:, None, :] * usage_now[None]
    low_usage = masked_usage.astype(bf16).reshape(dataset_count * factor_rank, slot_count)
    cross_stat_part = lax.dot_general(
        low_usage, expression, (((1,), (1,)), ((), ())), preferred_element_type=f32
    ).reshape(dataset_count, factor_rank, gene_count)
    cross_stat_part = cross_stat_part / counted[:, None, None]
    gram_stat_part = (
        jnp.einsum("dkc,dlc->dkl", masked_usage, masked_usage, precision=precise)
        / counted[:, None, None]
    )
    stat_cross, stat_gram = lax.psum((cross_stat_part, gram_stat_part), "cell")
    total_cross = jnp.sum(stat_cross, axis=0)
    total_gram = jnp.sum(stat_gram, axis=0)
    factor_now = dataset_factors
    for sweep in range(ITERS):
        divisor = jnp.einsum("dkl,lg->dkg", stat_gram, shared_factor, precision=precise) + (
            1.0 + penalty
        ) * jnp.einsum("dkl,dlg->dkg", stat_gram, factor_now, precision=precise)
        factor_now = factor_now * stat_cross / divisor
    total_pull = jnp.einsum("dkl,dlg->kg", stat_gram, factor_now, precision=precise)
    total_cross, total_gram, total_pull = lax.psum((total_cross, total_gram, total_pull), "dp")
    shared_now = shared_update(shared_factor, total_cross, total_gram, total_pull)
    return (usage_now, factor_now, shared_now)


def halves(value):
    high = value.astype(bf16)
    low = (value - high.astype(f32)).astype(bf16)
    return high, low


def nt_dot(a, b):
    return lax.dot_general(a, b, (((1,), (1,)), ((), ())), preferred_element_type=f32)


def left_cat(matrix):
    high, low = halves(matrix)
    return jnp.concatenate([high, low, high], axis=1)


def right_cat(value):
    high, low = halves(value)
    return jnp.concatenate([high, high, low], axis=0)


def flatten(block, width):
    parts = width // block.shape[1]
    rows = block.shape[0] // parts
    return jnp.concatenate([block[i * rows : (i + 1) * rows] for i in range(parts)], axis=1)


def unflatten(flat, rank):
    parts = flat.shape[1] // rank
    return jnp.concatenate([flat[:, i * rank : (i + 1) * rank] for i in range(parts)], axis=0)


def start_kernel(
    index_ref, shared_hbm, factors_hbm, expression_hbm, label_ref, send_ref, keep_ref,
    shared_ref, factors_ref, tile_ref, low_ref, sems,
):
    count, rank, genes = factors_ref.shape
    tiles, _, width = tile_ref.shape
    core = index_ref[0]

    def first_cell(t):
        which = jnp.where(t < tiles // 2, 1 - core, core) * (tiles // 2) + t % (tiles // 2)
        return pl.multiple_of(which * width, width)

    def tile_copy(t):
        return pltpu.make_async_copy(
            expression_hbm.at[:, pl.ds(first_cell(t), width)], tile_ref.at[t], sems.at[1 + count + t]
        )

    def factor_copy(e):
        return pltpu.make_async_copy(factors_hbm.at[e], factors_ref.at[e], sems.at[1 + e])

    shared_copy = pltpu.make_async_copy(shared_hbm, shared_ref, sems.at[0])
    shared_copy.start()
    for e in range(count):
        factor_copy(e).start()
    tile_copy(0).start()
    shared_copy.wait()
    for e in range(count):
        factor_copy(e).wait()
    for t in range(1, tiles):
        tile_copy(t).start()
    shared = shared_ref[...]
    low_ref[:rank, :] = shared.astype(bf16)
    out_width = send_ref.shape[1]
    rows = rank * rank // out_width
    for e in range(count):
        own = factors_ref[e]
        own_high, own_low = halves(own)
        both_high, both_low = halves(shared + own)
        low_ref[(e + 1) * rank : (e + 2) * rank, :] = own_high
        result = nt_dot(
            jnp.concatenate([both_high, own_high], axis=0),
            jnp.concatenate([both_high, both_low, own_high, own_low], axis=0),
        )
        mixed = result[:rank, rank : 2 * rank] + penalty * result[rank:, 3 * rank :]
        block = result[:rank, :rank] + penalty * result[rank:, 2 * rank : 3 * rank]
        flat = flatten(block + mixed + mixed.T, out_width)
        send_ref[rank + e * rows : rank + (e + 1) * rows, :] = flat
        keep_ref[rank + e * rows : rank + (e + 1) * rows, :] = flat

    for t in range(tiles):
        tile_copy(t).wait()
        products = jnp.dot(low_ref[...], tile_ref[t], preferred_element_type=f32)
        label = label_ref[:, pl.ds(first_cell(t), width)]
        total = products[:rank]
        for e in range(count):
            total += jnp.where(label == e, products[(e + 1) * rank : (e + 2) * rank], 0.0)
        out = send_ref if t < tiles // 2 else keep_ref
        at = t % (tiles // 2) * width
        out[:rank, at : at + width] = total


def usage_kernel(index_ref, own_ref, other_ref, usage_ref, label_ref, out_ref):
    rank = usage_ref.shape[0]
    both = own_ref[...] + other_ref[...]
    cross = both[:rank]
    rows = rank * rank // both.shape[1]
    count = both.shape[0] // rows - rank // rows
    left = left_cat(
        jnp.concatenate(
            [unflatten(both[rank + e * rows : rank + (e + 1) * rows], rank) for e in range(count)],
            axis=0,
        )
    )
    label = label_ref[...]
    alive = label < count
    usage = usage_ref[...]
    for sweep in range(ITERS):
        stacked = jnp.dot(left, right_cat(usage), preferred_element_type=f32)
        divisor = jnp.where(alive, 0.0, 1.0)
        for e in range(count):
            divisor += jnp.where(label == e, stacked[e * rank : (e + 1) * rank], 0.0)
        usage = jnp.where(alive, usage * cross / divisor, usage)
    out_ref[...] = usage


def usage_gram_kernel(index_ref, place_ref, own_ref, other_ref, label_ref, usage_ref, gram_ref, low_ref):
    rank, half = own_ref.shape
    count = low_ref.shape[0] // rank
    core = index_ref[0]
    usage_ref[:, pl.ds(pl.multiple_of(core * half, half), half)] = own_ref[...]
    usage_ref[:, pl.ds(pl.multiple_of((1 - core) * half, half), half)] = other_ref[...]
    usage = usage_ref[...]
    label = label_ref[...]
    high, low = halves(usage)
    right = jnp.concatenate([high, low], axis=0)
    columns = gram_ref.shape[1]
    for e in range(count):
        rows = slice(e * rank, (e + 1) * rank)
        masked = jnp.where(label == e, high, jnp.zeros_like(high))
        low_ref[rows, :] = masked
        both = nt_dot(masked, right)
        mixed = both[:, rank:]
        gram = both[:, :rank] + mixed + mixed.T
        share = gram[:, :columns]
        for k in range(1, rank // columns):
            share = jnp.where(place_ref[0] == k, gram[:, k * columns : (k + 1) * columns], share)
        gram_ref[rows, :] = share


def stat_kernel(low_ref, gram_ref, expression_ref, *parts):
    step = pl.program_id(0)
    result = nt_dot(low_ref[...], expression_ref[...])
    for t, ref in enumerate(parts):
        @pl.when(step == t)
        def _():
            ref[...] = result
            if t == 0:
                ref[:, -SPARE : gram_ref.shape[1] - SPARE] = gram_ref[...]


def gram_total_kernel(place_ref, size_ref, pair_ref, other_ref, left_ref, total_ref):
    width = total_ref.shape[1]
    rank = left_ref.shape[1] // 3
    count = left_ref.shape[0] // rank
    columns = pair_ref.shape[1] // 2
    place = place_ref[0]
    shares = [
        pair_ref[:, :columns], pair_ref[:, columns:], other_ref[:, :columns], other_ref[:, columns:]
    ]
    whole_gram = []
    for k in range(rank // columns):
        share = shares[0]
        for offset in range(1, rank // columns):
            share = jnp.where(place == k ^ offset, shares[offset], share)
        whole_gram.append(share)
    gram = jnp.concatenate(whole_gram, axis=1)
    total = jnp.zeros((rank, rank), f32)
    for e in range(count):
        rows = slice(e * rank, (e + 1) * rank)
        scaled = gram[rows] / size_ref[e].astype(f32)
        left_ref[rows, :] = left_cat(scaled)
        total += scaled
    total_ref[...] = flatten(total, width)


def factor_kernel(size_ref, cross_ref, left_ref, gram_ref, shared_ref, factors_ref, *rest):
    out_ref, total_ref = rest[-2:]
    count, rank, width = factors_ref.shape
    shared = shared_ref[...]
    lefts = [left_ref[e * rank : (e + 1) * rank, :] for e in range(count)]
    crosses = [
        cross_ref[e * rank : (e + 1) * rank, :] * (1.0 / size_ref[e].astype(f32))
        for e in range(count)
    ]
    factors = [factors_ref[e] for e in range(count)]
    for sweep in range(ITERS):
        divisors = [
            jnp.dot(
                lefts[e],
                right_cat(shared + (1.0 + penalty) * factors[e]),
                preferred_element_type=f32,
            )
            for e in range(count)
        ]
        factors = [factors[e] * crosses[e] / divisors[e] for e in range(count)]
    total_cross = jnp.zeros((rank, width), f32)
    total_pull = jnp.zeros((rank, width), f32)
    for e in range(count):
        out_ref[e] = factors[e]
        total_cross += crosses[e]
        total_pull += jnp.dot(lefts[e], right_cat(factors[e]), preferred_element_type=f32)
    total_ref[:rank, :] = total_cross
    total_ref[rank : 2 * rank, :] = total_pull
    if total_ref.shape[0] > 2 * rank:
        total_ref[2 * rank :, :] = gram_ref[...]


def shared_kernel(own_ref, other_ref, gram_own, gram_other, shared_ref, *rest):
    out_ref = rest[-1]
    rank = out_ref.shape[0]
    total = own_ref[...] + other_ref[...]
    left = left_cat(unflatten(gram_own[...] + gram_other[...], rank))
    shared = shared_ref[...]
    for sweep in range(ITERS):
        divisor = jnp.dot(left, right_cat(shared), preferred_element_type=f32) + total[rank : 2 * rank]
        shared = shared * total[:rank] / divisor
    out_ref[...] = shared


def struct(*shape, dtype=f32):
    return jax.ShapeDtypeStruct(shape, dtype)


def whole(shape):
    return pl.BlockSpec(shape, lambda *_: (0,) * len(shape))


def call(
    kernel, index, args, in_specs, out_shape, out_specs,
    grid=(1,), scratch=(), cost=None, aliases={}, vmem=16,
):
    return pl.pallas_call(
        kernel,
        grid_spec=pltpu.PrefetchScalarGridSpec(
            num_scalar_prefetch=len(index),
            grid=grid,
            in_specs=in_specs,
            out_specs=out_specs,
            scratch_shapes=list(scratch),
        ),
        out_shape=out_shape,
        compiler_params=pltpu.CompilerParams(vmem_limit_bytes=int(vmem * 1024 * 1024)),
        cost_estimate=cost,
        input_output_aliases=aliases,
    )(*index, *args)


def cost(flops, moved):
    return pl.CostEstimate(flops=int(flops), bytes_accessed=int(moved), transcendentals=0)


def swap(value, axis, offset, size):
    return lax.ppermute(value, axis, [(i, i ^ offset) for i in range(size)])


INWARD = [(0, 1), (3, 2)]
ACROSS = [(1, 2), (2, 1)]
OUTWARD = [(1, 0), (2, 3)]


ORDER = (
    ("across", 0),
    ("across", 1),
    ("outward", 0),
    ("across", 2),
    ("outward", 1),
    ("across", 3),
    ("gram", 0),
    ("outward", 2),
    ("gram_total", 0),
    ("outward", 3),
    ("factor", 0),
    ("factor", 1),
    ("factor", 2),
    ("shared", 0),
    ("shared", 1),
    ("factor", 3),
    ("shared", 2),
    ("shared", 3),
)


def fast_body(expression, usage_init, shared_factor, dataset_factors, cell_dataset, dataset_sizes):
    count, rank, genes = dataset_factors.shape
    cells = expression.shape[1]
    half = cells // 2
    tile = GENE_TILE
    core = lax.axis_index("gene") % 2
    index = core.astype(jnp.int32).reshape(1)
    place = lax.axis_index("gene").astype(jnp.int32).reshape(1)
    label = cell_dataset.reshape(1, cells)
    rows = count * rank
    flat = rank * rank // tile

    hbm = pl.BlockSpec(memory_space=pltpu.HBM)
    cell_tile = 512
    shape = (rank + count * rank * rank // half, half)
    send, keep = call(
        start_kernel,
        (index,),
        (shared_factor, dataset_factors, expression, label),
        [hbm, hbm, hbm, whole((1, cells))],
        [struct(*shape), struct(*shape)],
        [whole(shape), whole(shape)],
        scratch=[
            pltpu.VMEM((rank, genes), f32),
            pltpu.VMEM((count, rank, genes), f32),
            pltpu.VMEM((cells // cell_tile, genes, cell_tile), bf16),
            pltpu.VMEM((rows + rank, genes), bf16),
            pltpu.SemaphoreType.DMA((1 + count + cells // cell_tile,)),
        ],
        vmem=63,
        cost=cost(2 * (count + 1) * rank * genes * cells, 2 * genes * cells),
    )
    both = keep + swap(send, "gene", 1, 4)
    both_more = swap(both, "gene", 2, 4)
    usage_half = call(
        usage_kernel,
        (index,),
        (both, both_more, usage_init, label),
        [
            whole(shape),
            whole(shape),
            pl.BlockSpec((rank, half), lambda i, idx: (0, idx[0])),
            pl.BlockSpec((1, half), lambda i, idx: (0, idx[0])),
        ],
        struct(rank, half),
        whole((rank, half)),
        cost=cost(2 * ITERS * 3 * count * rank * rank * half, 16 * rank * half),
    )
    usage_other = swap(usage_half, "gene", 1, 4)

    pieces = pl.cdiv(genes, tile)
    columns = rank // 4
    usage, gram_share, low = call(
        usage_gram_kernel,
        (index, place),
        (usage_half, usage_other, label),
        [whole((rank, half)), whole((rank, half)), whole((1, cells))],
        [struct(rank, cells), struct(rows, columns), struct(rows, cells, dtype=bf16)],
        [whole((rank, cells)), whole((rows, columns)), whole((rows, cells))],
        cost=cost(4 * 2 * rows * rank * cells, 6 * rows * cells),
    )
    own = list(
        call(
            stat_kernel,
            (),
            (low, gram_share, expression),
            [
                whole((rows, cells)),
                whole((rows, columns)),
                pl.BlockSpec((tile, cells), lambda i: ((i + pieces - 1) % pieces, 0)),
            ],
            [struct(rows, tile)] * pieces,
            [whole((rows, tile))] * pieces,
            grid=(pieces,),
            cost=cost(2 * rows * genes * cells, 2 * genes * cells),
        )
    )

    inward = [lax.ppermute(part, "cell", INWARD) for part in own]
    across = [None] * pieces
    outward = [None] * pieces
    totals = [None] * pieces
    token = own[1]

    def after(token, *values):
        *values, token = lax.optimization_barrier((*values, token))
        return values

    new_factors = None
    new_shared = None
    gram_left = None
    grams = None
    gram_own = None

    def factor_call(j, total, into, flat_rows):
        gene_block = pl.BlockSpec((rank, tile), lambda i, idx: (0, j))
        set_block = pl.BlockSpec((count, rank, tile), lambda i, idx: (0, 0, j))
        more = () if into is None else (into,)
        shape = (2 * rank + flat_rows, tile)
        return call(
            factor_kernel,
            (dataset_sizes,),
            (total, gram_left, gram_own, shared_factor, dataset_factors) + more,
            [whole((rows, tile)), whole((rows, 3 * rank)), whole((flat, tile))]
            + [gene_block, set_block]
            + [pl.BlockSpec(memory_space=pl.ANY)] * len(more),
            [struct(count, rank, genes), struct(*shape)],
            [set_block, whole(shape)],
            aliases={6: 0} if more else {},
            cost=cost(2 * 4 * 3 * rows * rank * tile, 3 * 4 * rows * tile),
        )

    def shared_call(j, own_total, other_total, into):
        shape = (2 * rank, tile)
        block = pl.BlockSpec((rank, tile), lambda i: (0, j))
        more = () if into is None else (into,)
        return call(
            shared_kernel,
            (),
            (own_total, other_total, *grams, shared_factor) + more,
            [whole(shape)] * 2
            + [whole((flat, tile))] * 2
            + [block]
            + [pl.BlockSpec(memory_space=pl.ANY)] * len(more),
            struct(rank, genes),
            block,
            aliases={5: 0} if more else {},
            cost=cost(2 * 3 * 3 * rank * rank * tile, 6 * 4 * rank * tile),
        )

    def factor_step(j, token, into):
        part, got1, got2, got3 = after(token, own[j], inward[j], across[j], outward[j])
        total = (part + got1) + (got2 + got3)
        into, own_total = factor_call((j + pieces - 1) % pieces, total, into, flat if j == 0 else 0)
        totals[j] = (own_total, swap(own_total, "dp", 1, 2))
        return into, own_total

    def shared_step(j, token, into):
        own_total, other_total = after(token, *totals[j])
        return shared_call(
            (j + pieces - 1) % pieces, own_total[: 2 * rank], other_total[: 2 * rank], into
        )

    for step in ORDER:
        kind, j = step
        if kind == "across":
            part, got = after(token, own[j], inward[j])
            token = part + got
            across[j] = lax.ppermute(token, "cell", ACROSS)
        elif kind == "outward":
            part, got = after(token, own[j], across[j])
            token = part + got
            outward[j] = lax.ppermute(token, "cell", OUTWARD)
        elif kind == "gram":
            part, got1, got2, got3 = after(token, own[0], inward[0], across[0], outward[0])
            lanes = slice(tile - SPARE, tile - SPARE + columns)
            share = (part[:, lanes] + got1[:, lanes]) + (got2[:, lanes] + got3[:, lanes])
            pair = jnp.concatenate([share, swap(share, "gene", 1, 4)], axis=1)
            pair_got = swap(pair, "gene", 2, 4)
            token = pair
        elif kind == "gram_total":
            pair, pair_got = after(token, pair, pair_got)
            gram_left, gram_own = call(
                gram_total_kernel,
                (place, dataset_sizes),
                (pair, pair_got),
                [whole((rows, 2 * columns))] * 2,
                [struct(rows, 3 * rank, dtype=bf16), struct(flat, tile)],
                [whole((rows, 3 * rank)), whole((flat, tile))],
            )
            token = gram_own
        elif kind == "factor":
            new_factors, token = factor_step(j, token, new_factors)
            if j == 0:
                grams = [value[2 * rank :] for value in totals[0]]
        else:
            new_shared = shared_step(j, token, new_shared)
            token = new_shared
    return usage, new_factors, new_shared


def solution(mesh):
    sizes = (mesh.shape["dp"], mesh.shape["cell"], mesh.shape["gene"])
    return jax.shard_map(
        fast_body if sizes == (2, 4, 4) else plain_body,
        mesh=mesh,
        in_specs=(
            P("gene", ("dp", "cell")),
            P(None, ("dp", "cell")),
            P(None, "gene"),
            P("dp", None, "gene"),
            P(("dp", "cell")),
            P("dp"),
        ),
        out_specs=(P(None, ("dp", "cell")), P("dp", None, "gene"), P(None, "gene")),
        check_vma=False,
    )
```

```python
import functools

import jax
import jax.numpy as jnp
from jax import lax
from jax.experimental import pallas as pl
from jax.experimental.pallas import tpu as pltpu
from jax.sharding import PartitionSpec as P

ITERS = 3
penalty = 5.0
precise = lax.Precision.HIGHEST
f32 = jnp.float32
bf16 = jnp.bfloat16

GENE_TILE = 256
SPARE = 24
VMEM = pl.BlockSpec(memory_space=pltpu.VMEM)


def shared_update(shared_now, total_cross, total_gram, total_pull):
    for sweep in range(ITERS):
        shared_now = (
            shared_now
            * total_cross
            / (jnp.dot(total_gram, shared_now, precision=precise) + total_pull)
        )
    return shared_now


def plain_body(expression, usage_init, shared_factor, dataset_factors, cell_dataset, dataset_sizes):
    dataset_count = dataset_factors.shape[0]
    factor_rank = shared_factor.shape[0]
    gene_count = shared_factor.shape[1]
    slot_count = expression.shape[1]
    counted = dataset_sizes.astype(f32)
    onehot = (cell_dataset[None, :] == jnp.arange(dataset_count, dtype=jnp.int32)[:, None]).astype(f32)
    alive_mask = cell_dataset < dataset_count
    stacked_low = jnp.concatenate([shared_factor[None], dataset_factors], axis=0).astype(bf16)
    products = jnp.dot(
        stacked_low.reshape((dataset_count + 1) * factor_rank, gene_count),
        expression,
        preferred_element_type=f32,
    ).reshape(dataset_count + 1, factor_rank, slot_count)
    cross_part = products[0] + jnp.sum(onehot[:, None, :] * products[1:], axis=0)
    combined = shared_factor[None] + dataset_factors
    gram_part = jnp.einsum(
        "dkg,dlg->dkl", combined, combined, precision=precise
    ) + penalty * jnp.einsum("dkg,dlg->dkl", dataset_factors, dataset_factors, precision=precise)
    cross_sum, gram_full = lax.psum((cross_part, gram_part), "gene")
    usage_now = usage_init
    for sweep in range(ITERS):
        stacked = jnp.dot(
            gram_full.reshape(dataset_count * factor_rank, factor_rank),
            usage_now,
            precision=precise,
        ).reshape(dataset_count, factor_rank, slot_count)
        divisor = jnp.sum(onehot[:, None, :] * stacked, axis=0)
        divisor = jnp.where(alive_mask[None, :], divisor, 1.0)
        usage_now = jnp.where(alive_mask[None, :], usage_now * cross_sum / divisor, usage_now)
    masked_usage = onehot[:, None, :] * usage_now[None]
    low_usage = masked_usage.astype(bf16).reshape(dataset_count * factor_rank, slot_count)
    cross_stat_part = lax.dot_general(
        low_usage, expression, (((1,), (1,)), ((), ())), preferred_element_type=f32
    ).reshape(dataset_count, factor_rank, gene_count)
    cross_stat_part = cross_stat_part / counted[:, None, None]
    gram_stat_part = (
        jnp.einsum("dkc,dlc->dkl", masked_usage, masked_usage, precision=precise)
        / counted[:, None, None]
    )
    stat_cross, stat_gram = lax.psum((cross_stat_part, gram_stat_part), "cell")
    total_cross = jnp.sum(stat_cross, axis=0)
    total_gram = jnp.sum(stat_gram, axis=0)
    factor_now = dataset_factors
    for sweep in range(ITERS):
        divisor = jnp.einsum("dkl,lg->dkg", stat_gram, shared_factor, precision=precise) + (
            1.0 + penalty
        ) * jnp.einsum("dkl,dlg->dkg", stat_gram, factor_now, precision=precise)
        factor_now = factor_now * stat_cross / divisor
    total_pull = jnp.einsum("dkl,dlg->kg", stat_gram, factor_now, precision=precise)
    total_cross, total_gram, total_pull = lax.psum((total_cross, total_gram, total_pull), "dp")
    shared_now = shared_update(shared_factor, total_cross, total_gram, total_pull)
    return (usage_now, factor_now, shared_now)


def halves(value):
    high = value.astype(bf16)
    low = (value - high.astype(f32)).astype(bf16)
    return high, low


def nt_dot(a, b):
    return lax.dot_general(a, b, (((1,), (1,)), ((), ())), preferred_element_type=f32)


def left_cat(matrix):
    high, low = halves(matrix)
    return jnp.concatenate([high, low, high], axis=1)


def right_cat(value):
    high, low = halves(value)
    return jnp.concatenate([high, high, low], axis=0)


def flatten(block, width):
    parts = width // block.shape[1]
    rows = block.shape[0] // parts
    return jnp.concatenate([block[i * rows : (i + 1) * rows] for i in range(parts)], axis=1)


def unflatten(flat, rank):
    parts = flat.shape[1] // rank
    return jnp.concatenate([flat[:, i * rank : (i + 1) * rank] for i in range(parts)], axis=0)


def start_kernel(
    index_ref, shared_hbm, factors_hbm, expression_hbm, label_ref, send_ref, keep_ref,
    shared_ref, factors_ref, tile_ref, low_ref, sems,
):
    count, rank, genes = factors_ref.shape
    tiles, _, width = tile_ref.shape
    core = index_ref[0]

    def first_cell(t):
        which = jnp.where(t < tiles // 2, 1 - core, core) * (tiles // 2) + t % (tiles // 2)
        return pl.multiple_of(which * width, width)

    def tile_copy(t):
        return pltpu.make_async_copy(
            expression_hbm.at[:, pl.ds(first_cell(t), width)], tile_ref.at[t], sems.at[1 + count + t]
        )

    def factor_copy(e):
        return pltpu.make_async_copy(factors_hbm.at[e], factors_ref.at[e], sems.at[1 + e])

    shared_copy = pltpu.make_async_copy(shared_hbm, shared_ref, sems.at[0])
    shared_copy.start()
    for e in range(count):
        factor_copy(e).start()
    tile_copy(0).start()
    shared_copy.wait()
    for e in range(count):
        factor_copy(e).wait()
    for t in range(1, tiles):
        tile_copy(t).start()
    shared = shared_ref[...]
    low_ref[:rank, :] = shared.astype(bf16)
    out_width = send_ref.shape[1]
    rows = rank * rank // out_width
    for e in range(count):
        own = factors_ref[e]
        own_high, own_low = halves(own)
        both_high, both_low = halves(shared + own)
        low_ref[(e + 1) * rank : (e + 2) * rank, :] = own_high
        result = nt_dot(
            jnp.concatenate([both_high, own_high], axis=0),
            jnp.concatenate([both_high, both_low, own_high, own_low], axis=0),
        )
        mixed = result[:rank, rank : 2 * rank] + penalty * result[rank:, 3 * rank :]
        block = result[:rank, :rank] + penalty * result[rank:, 2 * rank : 3 * rank]
        flat = flatten(block + mixed + mixed.T, out_width)
        send_ref[rank + e * rows : rank + (e + 1) * rows, :] = flat
        keep_ref[rank + e * rows : rank + (e + 1) * rows, :] = flat

    for t in range(tiles):
        tile_copy(t).wait()
        products = jnp.dot(low_ref[...], tile_ref[t], preferred_element_type=f32)
        label = label_ref[:, pl.ds(first_cell(t), width)]
        total = products[:rank]
        for e in range(count):
            total += jnp.where(label == e, products[(e + 1) * rank : (e + 2) * rank], 0.0)
        out = send_ref if t < tiles // 2 else keep_ref
        at = t % (tiles // 2) * width
        out[:rank, at : at + width] = total


def usage_kernel(index_ref, own_ref, other_ref, usage_ref, label_ref, out_ref):
    rank = usage_ref.shape[0]
    both = own_ref[...] + other_ref[...]
    cross = both[:rank]
    rows = rank * rank // both.shape[1]
    count = both.shape[0] // rows - rank // rows
    left = left_cat(
        jnp.concatenate(
            [unflatten(both[rank + e * rows : rank + (e + 1) * rows], rank) for e in range(count)],
            axis=0,
        )
    )
    label = label_ref[...]
    alive = label < count
    usage = usage_ref[...]
    for sweep in range(ITERS):
        stacked = jnp.dot(left, right_cat(usage), preferred_element_type=f32)
        divisor = jnp.where(alive, 0.0, 1.0)
        for e in range(count):
            divisor += jnp.where(label == e, stacked[e * rank : (e + 1) * rank], 0.0)
        usage = jnp.where(alive, usage * cross / divisor, usage)
    out_ref[...] = usage


def usage_gram_kernel(index_ref, place_ref, own_ref, other_ref, label_ref, usage_ref, gram_ref, low_ref):
    rank, half = own_ref.shape
    count = low_ref.shape[0] // rank
    core = index_ref[0]
    usage_ref[:, pl.ds(pl.multiple_of(core * half, half), half)] = own_ref[...]
    usage_ref[:, pl.ds(pl.multiple_of((1 - core) * half, half), half)] = other_ref[...]
    usage = usage_ref[...]
    label = label_ref[...]
    high, low = halves(usage)
    right = jnp.concatenate([high, low], axis=0)
    columns = gram_ref.shape[1]
    for e in range(count):
        rows = slice(e * rank, (e + 1) * rank)
        masked = jnp.where(label == e, high, jnp.zeros_like(high))
        low_ref[rows, :] = masked
        both = nt_dot(masked, right)
        mixed = both[:, rank:]
        gram = both[:, :rank] + mixed + mixed.T
        share = gram[:, :columns]
        for k in range(1, rank // columns):
            share = jnp.where(place_ref[0] == k, gram[:, k * columns : (k + 1) * columns], share)
        gram_ref[rows, :] = share


def first_stat_kernel(low_ref, gram_ref, expression_ref, part_ref):
    part_ref[...] = nt_dot(low_ref[...], expression_ref[...])
    part_ref[:, -SPARE : gram_ref.shape[1] - SPARE] = gram_ref[...]


def stat_kernel(low_ref, expression_ref, *parts):
    step = pl.program_id(0)
    result = nt_dot(low_ref[...], expression_ref[...])
    for t, ref in enumerate(parts):
        @pl.when(step == t)
        def _():
            ref[...] = result


def gram_total_kernel(place_ref, size_ref, pair_ref, other_ref, left_ref, total_ref):
    width = total_ref.shape[1]
    rank = left_ref.shape[1] // 3
    count = left_ref.shape[0] // rank
    columns = pair_ref.shape[1] // 2
    place = place_ref[0]
    shares = [
        pair_ref[:, :columns], pair_ref[:, columns:], other_ref[:, :columns], other_ref[:, columns:]
    ]
    whole_gram = []
    for k in range(rank // columns):
        share = shares[0]
        for offset in range(1, rank // columns):
            share = jnp.where(place == k ^ offset, shares[offset], share)
        whole_gram.append(share)
    gram = jnp.concatenate(whole_gram, axis=1)
    total = jnp.zeros((rank, rank), f32)
    for e in range(count):
        rows = slice(e * rank, (e + 1) * rank)
        scaled = gram[rows] / size_ref[e].astype(f32)
        left_ref[rows, :] = left_cat(scaled)
        total += scaled
    total_ref[...] = flatten(total, width)


def factor_kernel(tiles, size_ref, *refs):
    crosses_ref, (left_ref, gram_ref, shared_ref, factors_ref) = refs[:tiles], refs[tiles : tiles + 4]
    out_ref, total_ref = refs[-2:]
    count, rank, width = factors_ref.shape
    shared = shared_ref[...]
    lefts = [left_ref[e * rank : (e + 1) * rank, :] for e in range(count)]
    crosses = [
        jnp.concatenate([ref[e * rank : (e + 1) * rank, :] for ref in crosses_ref], axis=1)
        * (1.0 / size_ref[e].astype(f32))
        for e in range(count)
    ]
    factors = [factors_ref[e] for e in range(count)]
    for sweep in range(ITERS):
        divisors = [
            jnp.dot(
                lefts[e],
                right_cat(shared + (1.0 + penalty) * factors[e]),
                preferred_element_type=f32,
            )
            for e in range(count)
        ]
        factors = [factors[e] * crosses[e] / divisors[e] for e in range(count)]
    total_cross = jnp.zeros((rank, width), f32)
    total_pull = jnp.zeros((rank, width), f32)
    for e in range(count):
        out_ref[e] = factors[e]
        total_cross += crosses[e]
        total_pull += jnp.dot(lefts[e], right_cat(factors[e]), preferred_element_type=f32)
    total_ref[:rank, :] = total_cross
    total_ref[rank : 2 * rank, :] = total_pull
    if total_ref.shape[0] > 2 * rank:
        total_ref[2 * rank :, : gram_ref.shape[1]] = gram_ref[...]
        total_ref[2 * rank :, gram_ref.shape[1] :] = jnp.zeros_like(gram_ref)


def shared_kernel(own_ref, other_ref, gram_own, gram_other, shared_ref, *rest):
    out_ref = rest[-1]
    rank = out_ref.shape[0]
    total = own_ref[...] + other_ref[...]
    left = left_cat(unflatten(gram_own[...] + gram_other[...], rank))
    shared = shared_ref[...]
    for sweep in range(ITERS):
        divisor = jnp.dot(left, right_cat(shared), preferred_element_type=f32) + total[rank : 2 * rank]
        shared = shared * total[:rank] / divisor
    out_ref[...] = shared


def struct(*shape, dtype=f32):
    return jax.ShapeDtypeStruct(shape, dtype)


def whole(shape):
    return pl.BlockSpec(shape, lambda *_: (0,) * len(shape))


def call(
    kernel, index, args, in_specs, out_shape, out_specs,
    grid=(1,), scratch=(), cost=None, aliases={}, vmem=16,
):
    return pl.pallas_call(
        kernel,
        grid_spec=pltpu.PrefetchScalarGridSpec(
            num_scalar_prefetch=len(index),
            grid=grid,
            in_specs=in_specs,
            out_specs=out_specs,
            scratch_shapes=list(scratch),
        ),
        out_shape=out_shape,
        compiler_params=pltpu.CompilerParams(vmem_limit_bytes=int(vmem * 1024 * 1024)),
        cost_estimate=cost,
        input_output_aliases=aliases,
    )(*index, *args)


def cost(flops, moved):
    return pl.CostEstimate(flops=int(flops), bytes_accessed=int(moved), transcendentals=0)


def swap(value, axis, offset, size):
    return lax.ppermute(value, axis, [(i, i ^ offset) for i in range(size)])


HALF_LINE = [(0, 1), (1, 0), (2, 3), (3, 2)]
ACROSS = [(4 * g + c, 4 * g + 3 - c) for g in (0, 1) for c in (1, 2)] + [
    (4 * g + c, 4 * (1 - g) + c) for g in (0, 1) for c in (0, 3)
]


ORDER = (
    ("across", 0),
    ("across", 1),
    ("outward", 0),
    ("across", 2),
    ("outward", 1),
    ("across", 3),
    ("gram", 0),
    ("outward", 2),
    ("sum", 1),
    ("gram_total", 0),
    ("outward", 3),
    ("factor", 0),
    ("factor", 2),
    ("factor", 3),
    ("shared", 0),
    ("shared", 2),
    ("shared", 3),
)


def fast_body(expression, usage_init, shared_factor, dataset_factors, cell_dataset, dataset_sizes):
    count, rank, genes = dataset_factors.shape
    cells = expression.shape[1]
    half = cells // 2
    tile = GENE_TILE
    core = lax.axis_index("gene") % 2
    index = core.astype(jnp.int32).reshape(1)
    place = lax.axis_index("gene").astype(jnp.int32).reshape(1)
    label = cell_dataset.reshape(1, cells)
    rows = count * rank
    flat = rank * rank // tile

    hbm = pl.BlockSpec(memory_space=pltpu.HBM)
    cell_tile = 512
    shape = (rank + count * rank * rank // half, half)
    send, keep = call(
        start_kernel,
        (index,),
        (shared_factor, dataset_factors, expression, label),
        [hbm, hbm, hbm, whole((1, cells))],
        [struct(*shape), struct(*shape)],
        [whole(shape), whole(shape)],
        scratch=[
            pltpu.VMEM((rank, genes), f32),
            pltpu.VMEM((count, rank, genes), f32),
            pltpu.VMEM((cells // cell_tile, genes, cell_tile), bf16),
            pltpu.VMEM((rows + rank, genes), bf16),
            pltpu.SemaphoreType.DMA((1 + count + cells // cell_tile,)),
        ],
        vmem=56,
        cost=cost(2 * (count + 1) * rank * genes * cells, 2 * genes * cells),
    )
    both = keep + swap(send, "gene", 1, 4)
    both_more = swap(both, "gene", 2, 4)
    usage_half = call(
        usage_kernel,
        (index,),
        (both, both_more, usage_init, label),
        [
            whole(shape),
            whole(shape),
            pl.BlockSpec((rank, half), lambda i, idx: (0, idx[0])),
            pl.BlockSpec((1, half), lambda i, idx: (0, idx[0])),
        ],
        struct(rank, half),
        whole((rank, half)),
        cost=cost(2 * ITERS * 3 * count * rank * rank * half, 16 * rank * half),
    )
    usage_other = swap(usage_half, "gene", 1, 4)

    pieces = pl.cdiv(genes, tile)
    columns = rank // 4
    usage, gram_share, low = call(
        usage_gram_kernel,
        (index, place),
        (usage_half, usage_other, label),
        [whole((rank, half)), whole((rank, half)), whole((1, cells))],
        [struct(rank, cells), struct(rows, columns), struct(rows, cells, dtype=bf16)],
        [whole((rank, cells)), whole((rows, columns)), whole((rows, cells))],
        cost=cost(4 * 2 * rows * rank * cells, 6 * rows * cells),
    )
    first = call(
        first_stat_kernel,
        (),
        (low, gram_share, expression),
        [
            whole((rows, cells)),
            whole((rows, columns)),
            pl.BlockSpec((tile, cells), lambda i: (pieces - 1, 0)),
        ],
        struct(rows, tile),
        whole((rows, tile)),
        cost=cost(2 * rows * tile * cells, 2 * tile * cells),
    )
    own = [first] + list(
        call(
            stat_kernel,
            (),
            (low, expression),
            [whole((rows, cells)), pl.BlockSpec((tile, cells), lambda i: (pieces - 2 - i, 0))],
            [struct(rows, tile)] * (pieces - 1),
            [whole((rows, tile))] * (pieces - 1),
            grid=(pieces - 1,),
            cost=cost(2 * rows * genes * cells, 2 * genes * cells),
        )
    )

    depth = lax.axis_index("cell")
    inner = (depth == 1) | (depth == 2)
    last = pieces - 1
    inward = [lax.ppermute(part, "cell", HALF_LINE) for part in own[:last]] + [None]
    across = [None] * pieces
    outward = [None] * pieces
    totals = [None] * pieces
    token = own[1]

    def after(token, *values):
        *values, token = lax.optimization_barrier((*values, token))
        return values

    new_factors = None
    new_shared = None
    gram_left = None
    grams = None
    gram_own = None

    def shared_call(block_at, width, own_total, other_total, into):
        shape = (2 * rank, width)
        block = pl.BlockSpec((rank, width), lambda i: (0, block_at))
        more = () if into is None else (into,)
        return call(
            shared_kernel,
            (),
            (own_total, other_total, *grams, shared_factor) + more,
            [whole(shape)] * 2
            + [whole((flat, tile))] * 2
            + [block]
            + [pl.BlockSpec(memory_space=pl.ANY)] * len(more),
            struct(rank, genes),
            block,
            aliases={5: 0} if more else {},
            cost=cost(2 * 3 * 3 * rank * rank * width, 6 * 4 * rank * width),
        )

    sums = [None] * pieces

    def sum_step(j, token):
        part, got1, got2, got3 = after(token, own[j], inward[j], across[j], outward[j])
        sums[j] = part + jnp.where(inner, got1 + got2, got3)
        return sums[j]

    def factor_step(first, number, token, into):
        width = number * tile
        block_at = (pieces - first - number) // number
        gene_block = pl.BlockSpec((rank, width), lambda i, idx: (0, block_at))
        set_block = pl.BlockSpec((count, rank, width), lambda i, idx: (0, 0, block_at))
        more = () if into is None else (into,)
        shape = (2 * rank + (flat if first == 0 else 0), width)
        *crosses, _ = lax.optimization_barrier((*sums[first : first + number][::-1], token))
        into, own_total = call(
            functools.partial(factor_kernel, number),
            (dataset_sizes,),
            (*crosses, gram_left, gram_own, shared_factor, dataset_factors) + more,
            [whole((rows, tile))] * number
            + [whole((rows, 3 * rank)), whole((flat, tile)), gene_block, set_block]
            + [pl.BlockSpec(memory_space=pl.ANY)] * len(more),
            [struct(count, rank, genes), struct(*shape)],
            [set_block, whole(shape)],
            aliases={5 + number: 0} if more else {},
            cost=cost(2 * 4 * 3 * rows * rank * width, 3 * 4 * rows * width),
        )
        totals[first] = (own_total, swap(own_total, "dp", 1, 2))
        return into, own_total

    def shared_step(first, number, token, into):
        own_total, other_total = after(token, *totals[first])
        return shared_call(
            (pieces - first - number) // number,
            number * tile,
            own_total[: 2 * rank],
            other_total[: 2 * rank],
            into,
        )

    for step in ORDER:
        kind, j = step
        if kind == "across":
            part, got = after(token, own[j], inward[j])
            token = part + got
            across[j] = lax.ppermute(token, ("dp", "cell"), ACROSS)
        elif kind == "outward":
            part, got = after(token, own[j], across[j])
            token = part + got
            if j == 0:
                mixed = jnp.where(inner, token, own[last])
                inward[last] = outward[0] = lax.ppermute(mixed, "cell", HALF_LINE)
            else:
                outward[j] = lax.ppermute(token, "cell", HALF_LINE)
        elif kind == "gram":
            part, got1, got2, got3 = after(token, own[0], inward[0], across[0], outward[0])
            lanes = slice(tile - SPARE, tile - SPARE + columns)
            share = part[:, lanes] + jnp.where(
                inner, got1[:, lanes] + got2[:, lanes], got3[:, lanes]
            )
            pair = jnp.concatenate([share, swap(share, "gene", 1, 4)], axis=1)
            pair_got = swap(pair, "gene", 2, 4)
            token = pair
        elif kind == "gram_total":
            pair, pair_got = after(token, pair, pair_got)
            gram_left, gram_own = call(
                gram_total_kernel,
                (place, dataset_sizes),
                (pair, pair_got),
                [whole((rows, 2 * columns))] * 2,
                [struct(rows, 3 * rank, dtype=bf16), struct(flat, tile)],
                [whole((rows, 3 * rank)), whole((flat, tile))],
            )
            token = gram_own
        elif kind == "sum":
            token = sum_step(j, token)
        elif kind == "factor":
            number = 2 if j == 0 else 1
            for k in range(j, j + number):
                if sums[k] is None:
                    sum_step(k, token)
            new_factors, token = factor_step(j, number, token, new_factors)
            if j == 0:
                grams = [value[2 * rank :, :tile] for value in totals[0]]
        else:
            new_shared = shared_step(j, 2 if j == 0 else 1, token, new_shared)
            token = new_shared
    return usage, new_factors, new_shared


def solution(mesh):
    sizes = (mesh.shape["dp"], mesh.shape["cell"], mesh.shape["gene"])
    return jax.shard_map(
        fast_body if sizes == (2, 4, 4) else plain_body,
        mesh=mesh,
        in_specs=(
            P("gene", ("dp", "cell")),
            P(None, ("dp", "cell")),
            P(None, "gene"),
            P("dp", None, "gene"),
            P(("dp", "cell")),
            P("dp"),
        ),
        out_specs=(P(None, ("dp", "cell")), P("dp", None, "gene"), P(None, "gene")),
        check_vma=False,
    )
```

```python
import functools

import jax
import jax.numpy as jnp
from jax import lax
from jax.experimental import pallas as pl
from jax.experimental.pallas import tpu as pltpu
from jax.sharding import PartitionSpec as P

ITERS = 3
penalty = 5.0
precise = lax.Precision.HIGHEST
f32 = jnp.float32
bf16 = jnp.bfloat16

GENE_TILE = 256
SPARE = 24
VMEM = pl.BlockSpec(memory_space=pltpu.VMEM)


def shared_update(shared_now, total_cross, total_gram, total_pull):
    for sweep in range(ITERS):
        shared_now = (
            shared_now
            * total_cross
            / (jnp.dot(total_gram, shared_now, precision=precise) + total_pull)
        )
    return shared_now


def plain_body(expression, usage_init, shared_factor, dataset_factors, cell_dataset, dataset_sizes):
    dataset_count = dataset_factors.shape[0]
    factor_rank = shared_factor.shape[0]
    gene_count = shared_factor.shape[1]
    slot_count = expression.shape[1]
    counted = dataset_sizes.astype(f32)
    onehot = (cell_dataset[None, :] == jnp.arange(dataset_count, dtype=jnp.int32)[:, None]).astype(f32)
    alive_mask = cell_dataset < dataset_count
    stacked_low = jnp.concatenate([shared_factor[None], dataset_factors], axis=0).astype(bf16)
    products = jnp.dot(
        stacked_low.reshape((dataset_count + 1) * factor_rank, gene_count),
        expression,
        preferred_element_type=f32,
    ).reshape(dataset_count + 1, factor_rank, slot_count)
    cross_part = products[0] + jnp.sum(onehot[:, None, :] * products[1:], axis=0)
    combined = shared_factor[None] + dataset_factors
    gram_part = jnp.einsum(
        "dkg,dlg->dkl", combined, combined, precision=precise
    ) + penalty * jnp.einsum("dkg,dlg->dkl", dataset_factors, dataset_factors, precision=precise)
    cross_sum, gram_full = lax.psum((cross_part, gram_part), "gene")
    usage_now = usage_init
    for sweep in range(ITERS):
        stacked = jnp.dot(
            gram_full.reshape(dataset_count * factor_rank, factor_rank),
            usage_now,
            precision=precise,
        ).reshape(dataset_count, factor_rank, slot_count)
        divisor = jnp.sum(onehot[:, None, :] * stacked, axis=0)
        divisor = jnp.where(alive_mask[None, :], divisor, 1.0)
        usage_now = jnp.where(alive_mask[None, :], usage_now * cross_sum / divisor, usage_now)
    masked_usage = onehot[:, None, :] * usage_now[None]
    low_usage = masked_usage.astype(bf16).reshape(dataset_count * factor_rank, slot_count)
    cross_stat_part = lax.dot_general(
        low_usage, expression, (((1,), (1,)), ((), ())), preferred_element_type=f32
    ).reshape(dataset_count, factor_rank, gene_count)
    cross_stat_part = cross_stat_part / counted[:, None, None]
    gram_stat_part = (
        jnp.einsum("dkc,dlc->dkl", masked_usage, masked_usage, precision=precise)
        / counted[:, None, None]
    )
    stat_cross, stat_gram = lax.psum((cross_stat_part, gram_stat_part), "cell")
    total_cross = jnp.sum(stat_cross, axis=0)
    total_gram = jnp.sum(stat_gram, axis=0)
    factor_now = dataset_factors
    for sweep in range(ITERS):
        divisor = jnp.einsum("dkl,lg->dkg", stat_gram, shared_factor, precision=precise) + (
            1.0 + penalty
        ) * jnp.einsum("dkl,dlg->dkg", stat_gram, factor_now, precision=precise)
        factor_now = factor_now * stat_cross / divisor
    total_pull = jnp.einsum("dkl,dlg->kg", stat_gram, factor_now, precision=precise)
    total_cross, total_gram, total_pull = lax.psum((total_cross, total_gram, total_pull), "dp")
    shared_now = shared_update(shared_factor, total_cross, total_gram, total_pull)
    return (usage_now, factor_now, shared_now)


def halves(value):
    high = value.astype(bf16)
    low = (value - high.astype(f32)).astype(bf16)
    return high, low


def nt_dot(a, b):
    return lax.dot_general(a, b, (((1,), (1,)), ((), ())), preferred_element_type=f32)


def left_cat(matrix):
    high, low = halves(matrix)
    return jnp.concatenate([high, low, high], axis=1)


def right_cat(value):
    high, low = halves(value)
    return jnp.concatenate([high, high, low], axis=0)


def flatten(block, width):
    parts = width // block.shape[1]
    rows = block.shape[0] // parts
    return jnp.concatenate([block[i * rows : (i + 1) * rows] for i in range(parts)], axis=1)


def unflatten(flat, rank):
    parts = flat.shape[1] // rank
    return jnp.concatenate([flat[:, i * rank : (i + 1) * rank] for i in range(parts)], axis=0)


def start_kernel(
    index_ref, shared_hbm, factors_hbm, expression_hbm, label_ref, send_ref, keep_ref,
    shared_ref, factors_ref, tile_ref, low_ref, sems,
):
    count, rank, genes = factors_ref.shape
    tiles, _, width = tile_ref.shape
    core = index_ref[0]

    def first_cell(t):
        which = jnp.where(t < tiles // 2, 1 - core, core) * (tiles // 2) + t % (tiles // 2)
        return pl.multiple_of(which * width, width)

    def tile_copy(t):
        return pltpu.make_async_copy(
            expression_hbm.at[:, pl.ds(first_cell(t), width)], tile_ref.at[t], sems.at[1 + count + t]
        )

    def factor_copy(e):
        return pltpu.make_async_copy(factors_hbm.at[e], factors_ref.at[e], sems.at[1 + e])

    shared_copy = pltpu.make_async_copy(shared_hbm, shared_ref, sems.at[0])
    shared_copy.start()
    for e in range(count):
        factor_copy(e).start()
    tile_copy(0).start()
    shared_copy.wait()
    for e in range(count):
        factor_copy(e).wait()
    for t in range(1, tiles):
        tile_copy(t).start()
    shared = shared_ref[...]
    shared_high, shared_low = halves(shared)
    low_ref[:rank, :] = shared_high
    pair = nt_dot(shared_high, jnp.concatenate([shared_high, shared_low], axis=0))
    shared_gram = pair[:, :rank] + pair[:, rank:] + pair[:, rank:].T
    out_width = send_ref.shape[1]
    rows = rank * rank // out_width
    for e in range(count):
        own = factors_ref[e]
        own_high, own_low = halves(own)
        low_ref[(e + 1) * rank : (e + 2) * rank, :] = own_high
        result = nt_dot(
            jnp.concatenate([shared_high, own_high], axis=0),
            jnp.concatenate([own_high, own_low, shared_low], axis=0),
        )
        cross = result[:rank, :rank] + result[:rank, rank : 2 * rank] + result[rank:, 2 * rank :].T
        mixed = cross + (1.0 + penalty) * result[rank:, rank : 2 * rank]
        block = shared_gram + (1.0 + penalty) * result[rank:, :rank]
        flat = flatten(block + mixed + mixed.T, out_width)
        send_ref[rank + e * rows : rank + (e + 1) * rows, :] = flat
        keep_ref[rank + e * rows : rank + (e + 1) * rows, :] = flat

    for t in range(tiles):
        tile_copy(t).wait()
        products = jnp.dot(low_ref[...], tile_ref[t], preferred_element_type=f32)
        label = label_ref[:, pl.ds(first_cell(t), width)]
        total = products[:rank]
        for e in range(count):
            total += jnp.where(label == e, products[(e + 1) * rank : (e + 2) * rank], 0.0)
        out = send_ref if t < tiles // 2 else keep_ref
        at = t % (tiles // 2) * width
        out[:rank, at : at + width] = total


def usage_kernel(index_ref, own_ref, other_ref, usage_ref, label_ref, out_ref):
    rank = usage_ref.shape[0]
    both = own_ref[...] + other_ref[...]
    cross = both[:rank]
    rows = rank * rank // both.shape[1]
    count = both.shape[0] // rows - rank // rows
    left = left_cat(
        jnp.concatenate(
            [unflatten(both[rank + e * rows : rank + (e + 1) * rows], rank) for e in range(count)],
            axis=0,
        )
    )
    label = label_ref[...]
    alive = label < count
    usage = usage_ref[...]
    for sweep in range(ITERS):
        stacked = jnp.dot(left, right_cat(usage), preferred_element_type=f32)
        divisor = jnp.where(alive, 0.0, 1.0)
        for e in range(count):
            divisor += jnp.where(label == e, stacked[e * rank : (e + 1) * rank], 0.0)
        usage = jnp.where(alive, usage * cross / divisor, usage)
    out_ref[...] = usage


def half_statistics(usage, label, expression, low_ref):
    rank, half = usage.shape
    count = low_ref.shape[0] // rank
    high, low = halves(usage)
    right = jnp.concatenate([high, low], axis=0)
    grams = []
    for e in range(count):
        masked = jnp.where(label == e, high, jnp.zeros_like(high))
        low_ref[e * rank : (e + 1) * rank, :] = masked
        grams.append(nt_dot(masked, right))
    return nt_dot(low_ref[...], expression), grams


def own_half_kernel(index_ref, own_ref, label_ref, expression_ref, low_ref, part_ref, gram_ref):
    rank = own_ref.shape[0]
    part, grams = half_statistics(own_ref[...], label_ref[...], expression_ref[...], low_ref)
    part_ref[...] = part
    for e, gram in enumerate(grams):
        gram_ref[e * rank : (e + 1) * rank, :] = gram


def first_stat_kernel(
    index_ref, place_ref, other_ref, own_part_ref, own_gram_ref, label_ref, expression_ref,
    low_ref, part_ref,
):
    rank, half = other_ref.shape
    count = low_ref.shape[0] // rank
    part, grams = half_statistics(other_ref[...], label_ref[...], expression_ref[...], low_ref)
    part_ref[...] = part + own_part_ref[...]
    columns = rank // 4
    for e in range(count):
        rows = slice(e * rank, (e + 1) * rank)
        both = grams[e] + own_gram_ref[rows, :]
        mixed = both[:, rank:]
        gram = both[:, :rank] + mixed + mixed.T
        share = gram[:, :columns]
        for k in range(1, rank // columns):
            share = jnp.where(place_ref[0] == k, gram[:, k * columns : (k + 1) * columns], share)
        part_ref[rows, -SPARE : columns - SPARE] = share


def stat_kernel(
    index_ref, own_ref, other_ref, low_ref, other_low_ref, expression_ref, other_expression_ref,
    usage_ref, *parts,
):
    step = pl.program_id(0)
    half = own_ref.shape[1]

    @pl.when(step == 0)
    def _():
        core = index_ref[0]
        usage_ref[:, pl.ds(pl.multiple_of(core * half, half), half)] = own_ref[...]
        usage_ref[:, pl.ds(pl.multiple_of((1 - core) * half, half), half)] = other_ref[...]

    result = nt_dot(low_ref[...], expression_ref[...])
    result += nt_dot(other_low_ref[...], other_expression_ref[...])
    for t, ref in enumerate(parts):
        @pl.when(step == t)
        def _():
            ref[...] = result


def gram_total_kernel(place_ref, size_ref, pair_ref, other_ref, left_ref, total_ref):
    width = total_ref.shape[1]
    rank = left_ref.shape[1] // 3
    count = left_ref.shape[0] // rank
    columns = pair_ref.shape[1] // 8
    packed = pair_ref.shape[0] // 2
    place = place_ref[0]
    shares = [
        jnp.concatenate(
            [
                ref[at : at + packed, i * columns : (i + 1) * columns]
                for i in range(8)
            ],
            axis=0,
        )
        for ref in (pair_ref, other_ref)
        for at in (0, packed)
    ]
    whole_gram = []
    for k in range(rank // columns):
        share = shares[0]
        for offset in range(1, rank // columns):
            share = jnp.where(place == k ^ offset, shares[offset], share)
        whole_gram.append(share)
    gram = jnp.concatenate(whole_gram, axis=1)
    total = jnp.zeros((rank, rank), f32)
    for e in range(count):
        rows = slice(e * rank, (e + 1) * rank)
        scaled = gram[rows] / size_ref[e].astype(f32)
        left_ref[rows, :] = left_cat(scaled)
        total += scaled
    total_ref[...] = flatten(total, width)


def factor_kernel(tiles, size_ref, *refs):
    crosses_ref, (left_ref, gram_ref, shared_ref, factors_ref) = refs[:tiles], refs[tiles : tiles + 4]
    out_ref, total_ref = refs[-2:]
    count, rank, width = factors_ref.shape
    shared = shared_ref[...]
    lefts = [left_ref[e * rank : (e + 1) * rank, :] for e in range(count)]
    crosses = [
        jnp.concatenate([ref[e * rank : (e + 1) * rank, :] for ref in crosses_ref], axis=1)
        * (1.0 / size_ref[e].astype(f32))
        for e in range(count)
    ]
    factors = [factors_ref[e] for e in range(count)]
    for sweep in range(ITERS):
        divisors = [
            jnp.dot(
                lefts[e],
                right_cat(shared + (1.0 + penalty) * factors[e]),
                preferred_element_type=f32,
            )
            for e in range(count)
        ]
        factors = [factors[e] * crosses[e] / divisors[e] for e in range(count)]
    total_cross = jnp.zeros((rank, width), f32)
    total_pull = jnp.zeros((rank, width), f32)
    for e in range(count):
        out_ref[e] = factors[e]
        total_cross += crosses[e]
        total_pull += jnp.dot(lefts[e], right_cat(factors[e]), preferred_element_type=f32)
    total_ref[:rank, :] = total_cross
    total_ref[rank : 2 * rank, :] = total_pull
    if total_ref.shape[0] > 2 * rank:
        total_ref[2 * rank :, : gram_ref.shape[1]] = gram_ref[...]
        total_ref[2 * rank :, gram_ref.shape[1] :] = jnp.zeros_like(gram_ref)


def shared_kernel(own_ref, other_ref, gram_own, gram_other, shared_ref, *rest):
    out_ref = rest[-1]
    rank = out_ref.shape[0]
    total = own_ref[...] + other_ref[...]
    left = left_cat(unflatten(gram_own[...] + gram_other[...], rank))
    shared = shared_ref[...]
    for sweep in range(ITERS):
        divisor = jnp.dot(left, right_cat(shared), preferred_element_type=f32) + total[rank : 2 * rank]
        shared = shared * total[:rank] / divisor
    out_ref[...] = shared


def struct(*shape, dtype=f32):
    return jax.ShapeDtypeStruct(shape, dtype)


def whole(shape):
    return pl.BlockSpec(shape, lambda *_: (0,) * len(shape))


def call(
    kernel, index, args, in_specs, out_shape, out_specs,
    grid=(1,), scratch=(), cost=None, aliases={}, vmem=16,
):
    return pl.pallas_call(
        kernel,
        grid_spec=pltpu.PrefetchScalarGridSpec(
            num_scalar_prefetch=len(index),
            grid=grid,
            in_specs=in_specs,
            out_specs=out_specs,
            scratch_shapes=list(scratch),
        ),
        out_shape=out_shape,
        compiler_params=pltpu.CompilerParams(vmem_limit_bytes=int(vmem * 1024 * 1024)),
        cost_estimate=cost,
        input_output_aliases=aliases,
    )(*index, *args)


def cost(flops, moved):
    return pl.CostEstimate(flops=int(flops), bytes_accessed=int(moved), transcendentals=0)


def swap(value, axis, offset, size):
    return lax.ppermute(value, axis, [(i, i ^ offset) for i in range(size)])


HALF_LINE = [(0, 1), (1, 0), (2, 3), (3, 2)]
ACROSS = [(4 * g + c, 4 * g + 3 - c) for g in (0, 1) for c in (1, 2)] + [
    (4 * g + c, 4 * (1 - g) + c) for g in (0, 1) for c in (0, 3)
]


ORDER = (
    ("across", 0),
    ("across", 1),
    ("outward", 0),
    ("across", 2),
    ("outward", 1),
    ("across", 3),
    ("gram", 0),
    ("outward", 2),
    ("sum", 1),
    ("gram_total", 0),
    ("factor", 0),
    ("outward", 3),
    ("factor", 2),
    ("factor", 3),
    ("shared", 0),
    ("shared", 2),
    ("shared", 3),
)


def fast_body(expression, usage_init, shared_factor, dataset_factors, cell_dataset, dataset_sizes):
    count, rank, genes = dataset_factors.shape
    cells = expression.shape[1]
    half = cells // 2
    tile = GENE_TILE
    core = lax.axis_index("gene") % 2
    index = core.astype(jnp.int32).reshape(1)
    place = lax.axis_index("gene").astype(jnp.int32).reshape(1)
    label = cell_dataset.reshape(1, cells)
    rows = count * rank
    flat = rank * rank // tile

    hbm = pl.BlockSpec(memory_space=pltpu.HBM)
    cell_tile = 512
    shape = (rank + count * rank * rank // half, half)
    send, keep = call(
        start_kernel,
        (index,),
        (shared_factor, dataset_factors, expression, label),
        [hbm, hbm, hbm, whole((1, cells))],
        [struct(*shape), struct(*shape)],
        [whole(shape), whole(shape)],
        scratch=[
            pltpu.VMEM((rank, genes), f32),
            pltpu.VMEM((count, rank, genes), f32),
            pltpu.VMEM((cells // cell_tile, genes, cell_tile), bf16),
            pltpu.VMEM((rows + rank, genes), bf16),
            pltpu.SemaphoreType.DMA((1 + count + cells // cell_tile,)),
        ],
        vmem=56,
        cost=cost(2 * (count + 1) * rank * genes * cells, 2 * genes * cells),
    )
    both = keep + swap(send, "gene", 1, 4)
    both_more = swap(both, "gene", 2, 4)
    usage_half = call(
        usage_kernel,
        (index,),
        (both, both_more, usage_init, label),
        [
            whole(shape),
            whole(shape),
            pl.BlockSpec((rank, half), lambda i, idx: (0, idx[0])),
            pl.BlockSpec((1, half), lambda i, idx: (0, idx[0])),
        ],
        struct(rank, half),
        whole((rank, half)),
        cost=cost(2 * ITERS * 3 * count * rank * rank * half, 16 * rank * half),
    )
    usage_other = swap(usage_half, "gene", 1, 4)

    pieces = pl.cdiv(genes, tile)
    columns = rank // 4
    low_half, part_half, gram_half = call(
        own_half_kernel,
        (index,),
        (usage_half, label, expression),
        [
            whole((rank, half)),
            pl.BlockSpec((1, half), lambda i, idx: (0, idx[0])),
            pl.BlockSpec((tile, half), lambda i, idx: (pieces - 1, idx[0])),
        ],
        [struct(rows, half, dtype=bf16), struct(rows, tile), struct(rows, 2 * rank)],
        [whole((rows, half)), whole((rows, tile)), whole((rows, 2 * rank))],
        cost=cost(2 * rows * (tile + 2 * rank) * half, 2 * tile * half),
    )
    other_low, first = call(
        first_stat_kernel,
        (index, place),
        (usage_other, part_half, gram_half, label, expression),
        [
            whole((rank, half)),
            whole((rows, tile)),
            whole((rows, 2 * rank)),
            pl.BlockSpec((1, half), lambda i, idx, _: (0, 1 - idx[0])),
            pl.BlockSpec((tile, half), lambda i, idx, _: (pieces - 1, 1 - idx[0])),
        ],
        [struct(rows, half, dtype=bf16), struct(rows, tile)],
        [whole((rows, half)), whole((rows, tile))],
        cost=cost(2 * rows * (tile + 2 * rank) * half, 2 * tile * half),
    )
    usage, *others = call(
        stat_kernel,
        (index,),
        (usage_half, usage_other, low_half, other_low, expression, expression),
        [
            whole((rank, half)),
            whole((rank, half)),
            whole((rows, half)),
            whole((rows, half)),
            pl.BlockSpec((tile, half), lambda i, idx: (pieces - 2 - i, idx[0])),
            pl.BlockSpec((tile, half), lambda i, idx: (pieces - 2 - i, 1 - idx[0])),
        ],
        [struct(rank, cells)] + [struct(rows, tile)] * (pieces - 1),
        [whole((rank, cells))] + [whole((rows, tile))] * (pieces - 1),
        grid=(pieces - 1,),
        cost=cost(2 * rows * genes * cells, 2 * genes * cells),
    )
    own = [first] + others

    depth = lax.axis_index("cell")
    inner = (depth == 1) | (depth == 2)
    last = pieces - 1
    inward = [lax.ppermute(part, "cell", HALF_LINE) for part in own[:last]] + [None]
    across = [None] * pieces
    outward = [None] * pieces
    totals = [None] * pieces
    token = own[1]

    def after(token, *values):
        *values, token = lax.optimization_barrier((*values, token))
        return values

    new_factors = None
    new_shared = None
    gram_left = None
    grams = None
    gram_own = None

    def shared_call(block_at, width, own_total, other_total, into):
        shape = (2 * rank, width)
        block = pl.BlockSpec((rank, width), lambda i: (0, block_at))
        more = () if into is None else (into,)
        return call(
            shared_kernel,
            (),
            (own_total, other_total, *grams, shared_factor) + more,
            [whole(shape)] * 2
            + [whole((flat, tile))] * 2
            + [block]
            + [pl.BlockSpec(memory_space=pl.ANY)] * len(more),
            struct(rank, genes),
            block,
            aliases={5: 0} if more else {},
            cost=cost(2 * 3 * 3 * rank * rank * width, 6 * 4 * rank * width),
        )

    sums = [None] * pieces

    def sum_step(j, token):
        part, got1, got2, got3 = after(token, own[j], inward[j], across[j], outward[j])
        sums[j] = part + jnp.where(inner, got1 + got2, got3)
        return sums[j]

    def factor_step(first, number, token, into):
        width = number * tile
        block_at = (pieces - first - number) // number
        gene_block = pl.BlockSpec((rank, width), lambda i, idx: (0, block_at))
        set_block = pl.BlockSpec((count, rank, width), lambda i, idx: (0, 0, block_at))
        more = () if into is None else (into,)
        shape = (2 * rank + (flat if first == 0 else 0), width)
        *crosses, _ = lax.optimization_barrier((*sums[first : first + number][::-1], token))
        into, own_total = call(
            functools.partial(factor_kernel, number),
            (dataset_sizes,),
            (*crosses, gram_left, gram_own, shared_factor, dataset_factors) + more,
            [whole((rows, tile))] * number
            + [whole((rows, 3 * rank)), whole((flat, tile)), gene_block, set_block]
            + [pl.BlockSpec(memory_space=pl.ANY)] * len(more),
            [struct(count, rank, genes), struct(*shape)],
            [set_block, whole(shape)],
            aliases={5 + number: 0} if more else {},
            cost=cost(2 * 4 * 3 * rows * rank * width, 3 * 4 * rows * width),
        )
        totals[first] = (own_total, swap(own_total, "dp", 1, 2))
        return into, own_total

    def shared_step(first, number, token, into):
        own_total, other_total = after(token, *totals[first])
        return shared_call(
            (pieces - first - number) // number,
            number * tile,
            own_total[: 2 * rank],
            other_total[: 2 * rank],
            into,
        )

    for step in ORDER:
        kind, j = step
        if kind == "across":
            part, got = after(token, own[j], inward[j])
            token = part + got
            across[j] = lax.ppermute(token, ("dp", "cell"), ACROSS)
        elif kind == "outward":
            part, got = after(token, own[j], across[j])
            token = part + got
            if j == 0:
                mixed = jnp.where(inner, token, own[last])
                inward[last] = outward[0] = lax.ppermute(mixed, "cell", HALF_LINE)
            else:
                outward[j] = lax.ppermute(token, "cell", HALF_LINE)
        elif kind == "gram":
            part, got1, got2, got3 = after(token, own[0], inward[0], across[0], outward[0])
            lanes = slice(tile - SPARE, tile - SPARE + columns)
            share = part[:, lanes] + jnp.where(
                inner, got1[:, lanes] + got2[:, lanes], got3[:, lanes]
            )
            packed = rows // 8
            share = jnp.concatenate(
                [share[i * packed : (i + 1) * packed] for i in range(8)], axis=1
            )
            pair = jnp.concatenate([share, swap(share, "gene", 1, 4)], axis=0)
            pair_got = swap(pair, "gene", 2, 4)
            token = pair
        elif kind == "gram_total":
            pair, pair_got = after(token, pair, pair_got)
            gram_left, gram_own = call(
                gram_total_kernel,
                (place, dataset_sizes),
                (pair, pair_got),
                [whole((2 * packed, 8 * columns))] * 2,
                [struct(rows, 3 * rank, dtype=bf16), struct(flat, tile)],
                [whole((rows, 3 * rank)), whole((flat, tile))],
                cost=cost(1000000, 200000),
            )
            token = gram_own
        elif kind == "sum":
            token = sum_step(j, token)
        elif kind == "factor":
            number = 2 if j == 0 else 1
            for k in range(j, j + number):
                if sums[k] is None:
                    sum_step(k, token)
            new_factors, token = factor_step(j, number, token, new_factors)
            if j == 0:
                grams = [value[2 * rank :, :tile] for value in totals[0]]
        else:
            new_shared = shared_step(j, 2 if j == 0 else 1, token, new_shared)
            token = new_shared
    return usage, new_factors, new_shared


def solution(mesh):
    sizes = (mesh.shape["dp"], mesh.shape["cell"], mesh.shape["gene"])
    return jax.shard_map(
        fast_body if sizes == (2, 4, 4) else plain_body,
        mesh=mesh,
        in_specs=(
            P("gene", ("dp", "cell")),
            P(None, ("dp", "cell")),
            P(None, "gene"),
            P("dp", None, "gene"),
            P(("dp", "cell")),
            P("dp"),
        ),
        out_specs=(P(None, ("dp", "cell")), P("dp", None, "gene"), P(None, "gene")),
        check_vma=False,
    )
```

```python
import functools

import jax
import jax.numpy as jnp
from jax import lax
from jax.experimental import pallas as pl
from jax.experimental.pallas import tpu as pltpu
from jax.sharding import PartitionSpec as P

ITERS = 3
penalty = 5.0
precise = lax.Precision.HIGHEST
f32 = jnp.float32
bf16 = jnp.bfloat16

GENE_TILE = 256
SPARE = 24
VMEM = pl.BlockSpec(memory_space=pltpu.VMEM)


def shared_update(shared_now, total_cross, total_gram, total_pull):
    for sweep in range(ITERS):
        shared_now = (
            shared_now
            * total_cross
            / (jnp.dot(total_gram, shared_now, precision=precise) + total_pull)
        )
    return shared_now


def plain_body(expression, usage_init, shared_factor, dataset_factors, cell_dataset, dataset_sizes):
    dataset_count = dataset_factors.shape[0]
    factor_rank = shared_factor.shape[0]
    gene_count = shared_factor.shape[1]
    slot_count = expression.shape[1]
    counted = dataset_sizes.astype(f32)
    onehot = (cell_dataset[None, :] == jnp.arange(dataset_count, dtype=jnp.int32)[:, None]).astype(f32)
    alive_mask = cell_dataset < dataset_count
    stacked_low = jnp.concatenate([shared_factor[None], dataset_factors], axis=0).astype(bf16)
    products = jnp.dot(
        stacked_low.reshape((dataset_count + 1) * factor_rank, gene_count),
        expression,
        preferred_element_type=f32,
    ).reshape(dataset_count + 1, factor_rank, slot_count)
    cross_part = products[0] + jnp.sum(onehot[:, None, :] * products[1:], axis=0)
    combined = shared_factor[None] + dataset_factors
    gram_part = jnp.einsum(
        "dkg,dlg->dkl", combined, combined, precision=precise
    ) + penalty * jnp.einsum("dkg,dlg->dkl", dataset_factors, dataset_factors, precision=precise)
    cross_sum, gram_full = lax.psum((cross_part, gram_part), "gene")
    usage_now = usage_init
    for sweep in range(ITERS):
        stacked = jnp.dot(
            gram_full.reshape(dataset_count * factor_rank, factor_rank),
            usage_now,
            precision=precise,
        ).reshape(dataset_count, factor_rank, slot_count)
        divisor = jnp.sum(onehot[:, None, :] * stacked, axis=0)
        divisor = jnp.where(alive_mask[None, :], divisor, 1.0)
        usage_now = jnp.where(alive_mask[None, :], usage_now * cross_sum / divisor, usage_now)
    masked_usage = onehot[:, None, :] * usage_now[None]
    low_usage = masked_usage.astype(bf16).reshape(dataset_count * factor_rank, slot_count)
    cross_stat_part = lax.dot_general(
        low_usage, expression, (((1,), (1,)), ((), ())), preferred_element_type=f32
    ).reshape(dataset_count, factor_rank, gene_count)
    cross_stat_part = cross_stat_part / counted[:, None, None]
    gram_stat_part = (
        jnp.einsum("dkc,dlc->dkl", masked_usage, masked_usage, precision=precise)
        / counted[:, None, None]
    )
    stat_cross, stat_gram = lax.psum((cross_stat_part, gram_stat_part), "cell")
    total_cross = jnp.sum(stat_cross, axis=0)
    total_gram = jnp.sum(stat_gram, axis=0)
    factor_now = dataset_factors
    for sweep in range(ITERS):
        divisor = jnp.einsum("dkl,lg->dkg", stat_gram, shared_factor, precision=precise) + (
            1.0 + penalty
        ) * jnp.einsum("dkl,dlg->dkg", stat_gram, factor_now, precision=precise)
        factor_now = factor_now * stat_cross / divisor
    total_pull = jnp.einsum("dkl,dlg->kg", stat_gram, factor_now, precision=precise)
    total_cross, total_gram, total_pull = lax.psum((total_cross, total_gram, total_pull), "dp")
    shared_now = shared_update(shared_factor, total_cross, total_gram, total_pull)
    return (usage_now, factor_now, shared_now)


def halves(value):
    high = value.astype(bf16)
    low = (value - high.astype(f32)).astype(bf16)
    return high, low


def nt_dot(a, b):
    return lax.dot_general(a, b, (((1,), (1,)), ((), ())), preferred_element_type=f32)


def left_cat(matrix):
    high, low = halves(matrix)
    return jnp.concatenate([high, low, high], axis=1)


def right_cat(value):
    high, low = halves(value)
    return jnp.concatenate([high, high, low], axis=0)


def thirds(value):
    high, rest = value.astype(bf16), value
    rest = rest - high.astype(f32)
    middle = rest.astype(bf16)
    low = (rest - middle.astype(f32)).astype(bf16)
    return high, middle, low


def fine_left(matrix):
    high, middle, low = thirds(matrix)
    return jnp.concatenate([high, high, middle, middle, high, low], axis=1)


def fine_right(value):
    high, middle, low = thirds(value)
    return jnp.concatenate([high, middle, high, middle, low, high], axis=0)


def flatten(block, width):
    parts = width // block.shape[1]
    rows = block.shape[0] // parts
    return jnp.concatenate([block[i * rows : (i + 1) * rows] for i in range(parts)], axis=1)


def unflatten(flat, rank):
    parts = flat.shape[1] // rank
    return jnp.concatenate([flat[:, i * rank : (i + 1) * rank] for i in range(parts)], axis=0)


def start_kernel(
    index_ref, shared_hbm, factors_hbm, expression_hbm, label_ref, send_ref, keep_ref,
    shared_ref, factors_ref, tile_ref, low_ref, sems,
):
    count, rank, genes = factors_ref.shape
    tiles, _, width = tile_ref.shape
    core = index_ref[0]

    def first_cell(t):
        which = jnp.where(t < tiles // 2, 1 - core, core) * (tiles // 2) + t % (tiles // 2)
        return pl.multiple_of(which * width, width)

    def tile_copy(t):
        return pltpu.make_async_copy(
            expression_hbm.at[:, pl.ds(first_cell(t), width)], tile_ref.at[t], sems.at[1 + count + t]
        )

    def factor_copy(e):
        return pltpu.make_async_copy(factors_hbm.at[e], factors_ref.at[e], sems.at[1 + e])

    shared_copy = pltpu.make_async_copy(shared_hbm, shared_ref, sems.at[0])
    shared_copy.start()
    for e in range(count):
        factor_copy(e).start()
    tile_copy(0).start()
    shared_copy.wait()
    for e in range(count):
        factor_copy(e).wait()
    for t in range(1, tiles):
        tile_copy(t).start()
    shared = shared_ref[...]
    shared_high, shared_low = halves(shared)
    low_ref[:rank, :] = shared_high
    pair = nt_dot(shared_high, jnp.concatenate([shared_high, shared_low], axis=0))
    shared_gram = pair[:, :rank] + pair[:, rank:] + pair[:, rank:].T
    out_width = send_ref.shape[1]
    rows = rank * rank // out_width
    for e in range(count):
        own = factors_ref[e]
        own_high, own_low = halves(own)
        low_ref[(e + 1) * rank : (e + 2) * rank, :] = own_high
        result = nt_dot(
            jnp.concatenate([shared_high, own_high], axis=0),
            jnp.concatenate([own_high, own_low, shared_low], axis=0),
        )
        cross = result[:rank, :rank] + result[:rank, rank : 2 * rank] + result[rank:, 2 * rank :].T
        mixed = cross + (1.0 + penalty) * result[rank:, rank : 2 * rank]
        block = shared_gram + (1.0 + penalty) * result[rank:, :rank]
        flat = flatten(block + mixed + mixed.T, out_width)
        send_ref[rank + e * rows : rank + (e + 1) * rows, :] = flat
        keep_ref[rank + e * rows : rank + (e + 1) * rows, :] = flat

    for t in range(tiles):
        tile_copy(t).wait()
        products = jnp.dot(low_ref[...], tile_ref[t], preferred_element_type=f32)
        label = label_ref[:, pl.ds(first_cell(t), width)]
        total = products[:rank]
        for e in range(count):
            total += jnp.where(label == e, products[(e + 1) * rank : (e + 2) * rank], 0.0)
        out = send_ref if t < tiles // 2 else keep_ref
        at = t % (tiles // 2) * width
        out[:rank, at : at + width] = total


def usage_kernel(index_ref, own_ref, other_ref, usage_ref, label_ref, out_ref):
    rank = usage_ref.shape[0]
    both = own_ref[...] + other_ref[...]
    cross = both[:rank]
    rows = rank * rank // both.shape[1]
    count = both.shape[0] // rows - rank // rows
    left = fine_left(
        jnp.concatenate(
            [unflatten(both[rank + e * rows : rank + (e + 1) * rows], rank) for e in range(count)],
            axis=0,
        )
    )
    label = label_ref[...]
    alive = label < count
    usage = usage_ref[...]
    for sweep in range(ITERS):
        stacked = jnp.dot(left, fine_right(usage), preferred_element_type=f32)
        divisor = jnp.where(alive, 0.0, 1.0)
        for e in range(count):
            divisor += jnp.where(label == e, stacked[e * rank : (e + 1) * rank], 0.0)
        usage = jnp.where(alive, usage * cross / divisor, usage)
    out_ref[...] = usage


def half_statistics(usage, label, expression, low_ref):
    rank, half = usage.shape
    count = low_ref.shape[0] // rank
    high, low = halves(usage)
    right = jnp.concatenate([high, low], axis=0)
    grams = []
    for e in range(count):
        masked = jnp.where(label == e, high, jnp.zeros_like(high))
        low_ref[e * rank : (e + 1) * rank, :] = masked
        grams.append(nt_dot(masked, right))
    return nt_dot(low_ref[...], expression), grams


def own_half_kernel(index_ref, own_ref, label_ref, expression_ref, low_ref, part_ref, gram_ref):
    rank = own_ref.shape[0]
    part, grams = half_statistics(own_ref[...], label_ref[...], expression_ref[...], low_ref)
    part_ref[...] = part
    for e, gram in enumerate(grams):
        gram_ref[e * rank : (e + 1) * rank, :] = gram


def first_stat_kernel(
    index_ref, place_ref, other_ref, own_part_ref, own_gram_ref, label_ref, expression_ref,
    low_ref, part_ref,
):
    rank, half = other_ref.shape
    count = low_ref.shape[0] // rank
    part, grams = half_statistics(other_ref[...], label_ref[...], expression_ref[...], low_ref)
    part_ref[...] = part + own_part_ref[...]
    columns = rank // 4
    for e in range(count):
        rows = slice(e * rank, (e + 1) * rank)
        both = grams[e] + own_gram_ref[rows, :]
        mixed = both[:, rank:]
        gram = both[:, :rank] + mixed + mixed.T
        share = gram[:, :columns]
        for k in range(1, rank // columns):
            share = jnp.where(place_ref[0] == k, gram[:, k * columns : (k + 1) * columns], share)
        part_ref[rows, -SPARE : columns - SPARE] = share


def stat_kernel(
    index_ref, own_ref, other_ref, low_ref, other_low_ref, expression_ref, other_expression_ref,
    usage_ref, *parts,
):
    step = pl.program_id(0)
    half = own_ref.shape[1]

    @pl.when(step == 0)
    def _():
        core = index_ref[0]
        usage_ref[:, pl.ds(pl.multiple_of(core * half, half), half)] = own_ref[...]
        usage_ref[:, pl.ds(pl.multiple_of((1 - core) * half, half), half)] = other_ref[...]

    result = nt_dot(low_ref[...], expression_ref[...])
    result += nt_dot(other_low_ref[...], other_expression_ref[...])
    for t, ref in enumerate(parts):
        @pl.when(step == t)
        def _():
            ref[...] = result


def gram_total_kernel(place_ref, size_ref, pair_ref, other_ref, left_ref, total_ref):
    width = total_ref.shape[1]
    rank = left_ref.shape[1] // 3
    count = left_ref.shape[0] // rank
    columns = pair_ref.shape[1] // 8
    packed = pair_ref.shape[0] // 2
    place = place_ref[0]
    shares = [
        jnp.concatenate(
            [
                ref[at : at + packed, i * columns : (i + 1) * columns]
                for i in range(8)
            ],
            axis=0,
        )
        for ref in (pair_ref, other_ref)
        for at in (0, packed)
    ]
    whole_gram = []
    for k in range(rank // columns):
        share = shares[0]
        for offset in range(1, rank // columns):
            share = jnp.where(place == k ^ offset, shares[offset], share)
        whole_gram.append(share)
    gram = jnp.concatenate(whole_gram, axis=1)
    total = jnp.zeros((rank, rank), f32)
    for e in range(count):
        rows = slice(e * rank, (e + 1) * rank)
        scaled = gram[rows] / size_ref[e].astype(f32)
        left_ref[rows, :] = left_cat(scaled)
        total += scaled
    total_ref[...] = flatten(total, width)


def factor_kernel(tiles, size_ref, *refs):
    crosses_ref, (left_ref, gram_ref, shared_ref, factors_ref) = refs[:tiles], refs[tiles : tiles + 4]
    out_ref, total_ref = refs[-2:]
    count, rank, width = factors_ref.shape
    shared = shared_ref[...]
    lefts = [left_ref[e * rank : (e + 1) * rank, :] for e in range(count)]
    crosses = [
        jnp.concatenate([ref[e * rank : (e + 1) * rank, :] for ref in crosses_ref], axis=1)
        * (1.0 / size_ref[e].astype(f32))
        for e in range(count)
    ]
    factors = [factors_ref[e] for e in range(count)]
    for sweep in range(ITERS):
        divisors = [
            jnp.dot(
                lefts[e],
                right_cat(shared + (1.0 + penalty) * factors[e]),
                preferred_element_type=f32,
            )
            for e in range(count)
        ]
        factors = [factors[e] * crosses[e] / divisors[e] for e in range(count)]
    total_cross = jnp.zeros((rank, width), f32)
    total_pull = jnp.zeros((rank, width), f32)
    for e in range(count):
        out_ref[e] = factors[e]
        total_cross += crosses[e]
        total_pull += jnp.dot(lefts[e], right_cat(factors[e]), preferred_element_type=f32)
    total_ref[:rank, :] = total_cross
    total_ref[rank : 2 * rank, :] = total_pull
    if total_ref.shape[0] > 2 * rank:
        total_ref[2 * rank :, : gram_ref.shape[1]] = gram_ref[...]
        total_ref[2 * rank :, gram_ref.shape[1] :] = jnp.zeros_like(gram_ref)


def shared_kernel(own_ref, other_ref, gram_own, gram_other, shared_ref, *rest):
    out_ref = rest[-1]
    rank = out_ref.shape[0]
    total = own_ref[...] + other_ref[...]
    left = left_cat(unflatten(gram_own[...] + gram_other[...], rank))
    shared = shared_ref[...]
    for sweep in range(ITERS):
        divisor = jnp.dot(left, right_cat(shared), preferred_element_type=f32) + total[rank : 2 * rank]
        shared = shared * total[:rank] / divisor
    out_ref[...] = shared


def struct(*shape, dtype=f32):
    return jax.ShapeDtypeStruct(shape, dtype)


def whole(shape):
    return pl.BlockSpec(shape, lambda *_: (0,) * len(shape))


def call(
    kernel, index, args, in_specs, out_shape, out_specs,
    grid=(1,), scratch=(), cost=None, aliases={}, vmem=16,
):
    return pl.pallas_call(
        kernel,
        grid_spec=pltpu.PrefetchScalarGridSpec(
            num_scalar_prefetch=len(index),
            grid=grid,
            in_specs=in_specs,
            out_specs=out_specs,
            scratch_shapes=list(scratch),
        ),
        out_shape=out_shape,
        compiler_params=pltpu.CompilerParams(vmem_limit_bytes=int(vmem * 1024 * 1024)),
        cost_estimate=cost,
        input_output_aliases=aliases,
    )(*index, *args)


def cost(flops, moved):
    return pl.CostEstimate(flops=int(flops), bytes_accessed=int(moved), transcendentals=0)


def swap(value, axis, offset, size):
    return lax.ppermute(value, axis, [(i, i ^ offset) for i in range(size)])


HALF_LINE = [(0, 1), (1, 0), (2, 3), (3, 2)]
ACROSS = [(4 * g + c, 4 * g + 3 - c) for g in (0, 1) for c in (1, 2)] + [
    (4 * g + c, 4 * (1 - g) + c) for g in (0, 1) for c in (0, 3)
]


ORDER = (
    ("across", 0),
    ("across", 1),
    ("outward", 0),
    ("across", 2),
    ("outward", 1),
    ("across", 3),
    ("gram", 0),
    ("outward", 2),
    ("sum", 1),
    ("gram_total", 0),
    ("factor", 0),
    ("outward", 3),
    ("factor", 2),
    ("factor", 3),
    ("shared", 0),
    ("shared", 2),
    ("shared", 3),
)


def fast_body(expression, usage_init, shared_factor, dataset_factors, cell_dataset, dataset_sizes):
    count, rank, genes = dataset_factors.shape
    cells = expression.shape[1]
    half = cells // 2
    tile = GENE_TILE
    core = lax.axis_index("gene") % 2
    index = core.astype(jnp.int32).reshape(1)
    place = lax.axis_index("gene").astype(jnp.int32).reshape(1)
    label = cell_dataset.reshape(1, cells)
    rows = count * rank
    flat = rank * rank // tile

    hbm = pl.BlockSpec(memory_space=pltpu.HBM)
    cell_tile = 512
    shape = (rank + count * rank * rank // half, half)
    send, keep = call(
        start_kernel,
        (index,),
        (shared_factor, dataset_factors, expression, label),
        [hbm, hbm, hbm, whole((1, cells))],
        [struct(*shape), struct(*shape)],
        [whole(shape), whole(shape)],
        scratch=[
            pltpu.VMEM((rank, genes), f32),
            pltpu.VMEM((count, rank, genes), f32),
            pltpu.VMEM((cells // cell_tile, genes, cell_tile), bf16),
            pltpu.VMEM((rows + rank, genes), bf16),
            pltpu.SemaphoreType.DMA((1 + count + cells // cell_tile,)),
        ],
        vmem=53.5,
        cost=cost(2 * (count + 1) * rank * genes * cells, 2 * genes * cells),
    )
    both = keep + swap(send, "gene", 1, 4)
    both_more = swap(both, "gene", 2, 4)
    usage_half = call(
        usage_kernel,
        (index,),
        (both, both_more, usage_init, label),
        [
            whole(shape),
            whole(shape),
            pl.BlockSpec((rank, half), lambda i, idx: (0, idx[0])),
            pl.BlockSpec((1, half), lambda i, idx: (0, idx[0])),
        ],
        struct(rank, half),
        whole((rank, half)),
        cost=cost(2 * ITERS * 3 * count * rank * rank * half, 16 * rank * half),
    )
    usage_other = swap(usage_half, "gene", 1, 4)

    pieces = pl.cdiv(genes, tile)
    columns = rank // 4
    low_half, part_half, gram_half = call(
        own_half_kernel,
        (index,),
        (usage_half, label, expression),
        [
            whole((rank, half)),
            pl.BlockSpec((1, half), lambda i, idx: (0, idx[0])),
            pl.BlockSpec((tile, half), lambda i, idx: (pieces - 1, idx[0])),
        ],
        [struct(rows, half, dtype=bf16), struct(rows, tile), struct(rows, 2 * rank)],
        [whole((rows, half)), whole((rows, tile)), whole((rows, 2 * rank))],
        cost=cost(2 * rows * (tile + 2 * rank) * half, 2 * tile * half),
    )
    other_low, first = call(
        first_stat_kernel,
        (index, place),
        (usage_other, part_half, gram_half, label, expression),
        [
            whole((rank, half)),
            whole((rows, tile)),
            whole((rows, 2 * rank)),
            pl.BlockSpec((1, half), lambda i, idx, _: (0, 1 - idx[0])),
            pl.BlockSpec((tile, half), lambda i, idx, _: (pieces - 1, 1 - idx[0])),
        ],
        [struct(rows, half, dtype=bf16), struct(rows, tile)],
        [whole((rows, half)), whole((rows, tile))],
        cost=cost(2 * rows * (tile + 2 * rank) * half, 2 * tile * half),
    )
    usage, *others = call(
        stat_kernel,
        (index,),
        (usage_half, usage_other, low_half, other_low, expression, expression),
        [
            whole((rank, half)),
            whole((rank, half)),
            whole((rows, half)),
            whole((rows, half)),
            pl.BlockSpec((tile, half), lambda i, idx: (pieces - 2 - i, idx[0])),
            pl.BlockSpec((tile, half), lambda i, idx: (pieces - 2 - i, 1 - idx[0])),
        ],
        [struct(rank, cells)] + [struct(rows, tile)] * (pieces - 1),
        [whole((rank, cells))] + [whole((rows, tile))] * (pieces - 1),
        grid=(pieces - 1,),
        cost=cost(2 * rows * genes * cells, 2 * genes * cells),
    )
    own = [first] + others

    depth = lax.axis_index("cell")
    inner = (depth == 1) | (depth == 2)
    last = pieces - 1
    inward = [lax.ppermute(part, "cell", HALF_LINE) for part in own[:last]] + [None]
    across = [None] * pieces
    outward = [None] * pieces
    totals = [None] * pieces
    token = own[1]

    def after(token, *values):
        *values, token = lax.optimization_barrier((*values, token))
        return values

    new_factors = None
    new_shared = None
    gram_left = None
    grams = None
    gram_own = None

    def shared_call(block_at, width, own_total, other_total, into):
        shape = (2 * rank, width)
        block = pl.BlockSpec((rank, width), lambda i: (0, block_at))
        more = () if into is None else (into,)
        return call(
            shared_kernel,
            (),
            (own_total, other_total, *grams, shared_factor) + more,
            [whole(shape)] * 2
            + [whole((flat, tile))] * 2
            + [block]
            + [pl.BlockSpec(memory_space=pl.ANY)] * len(more),
            struct(rank, genes),
            block,
            aliases={5: 0} if more else {},
            cost=cost(2 * 3 * 3 * rank * rank * width, 6 * 4 * rank * width),
        )

    sums = [None] * pieces

    def sum_step(j, token):
        part, got1, got2, got3 = after(token, own[j], inward[j], across[j], outward[j])
        sums[j] = part + jnp.where(inner, got1 + got2, got3)
        return sums[j]

    def factor_step(first, number, token, into):
        width = number * tile
        block_at = (pieces - first - number) // number
        gene_block = pl.BlockSpec((rank, width), lambda i, idx: (0, block_at))
        set_block = pl.BlockSpec((count, rank, width), lambda i, idx: (0, 0, block_at))
        more = () if into is None else (into,)
        shape = (2 * rank + (flat if first == 0 else 0), width)
        *crosses, _ = lax.optimization_barrier((*sums[first : first + number][::-1], token))
        into, own_total = call(
            functools.partial(factor_kernel, number),
            (dataset_sizes,),
            (*crosses, gram_left, gram_own, shared_factor, dataset_factors) + more,
            [whole((rows, tile))] * number
            + [whole((rows, 3 * rank)), whole((flat, tile)), gene_block, set_block]
            + [pl.BlockSpec(memory_space=pl.ANY)] * len(more),
            [struct(count, rank, genes), struct(*shape)],
            [set_block, whole(shape)],
            aliases={5 + number: 0} if more else {},
            cost=cost(2 * 4 * 3 * rows * rank * width, 3 * 4 * rows * width),
        )
        totals[first] = (own_total, swap(own_total, "dp", 1, 2))
        return into, own_total

    def shared_step(first, number, token, into):
        own_total, other_total = after(token, *totals[first])
        return shared_call(
            (pieces - first - number) // number,
            number * tile,
            own_total[: 2 * rank],
            other_total[: 2 * rank],
            into,
        )

    for step in ORDER:
        kind, j = step
        if kind == "across":
            part, got = after(token, own[j], inward[j])
            both = part + got
            across[j] = lax.ppermute(both, ("dp", "cell"), ACROSS)
            token = both if j == 2 else got
        elif kind == "outward":
            part, got = after(token, own[j], across[j])
            both, token = part + got, got
            if j == 0:
                mixed = jnp.where(inner, both, own[last])
                inward[last] = outward[0] = lax.ppermute(mixed, "cell", HALF_LINE)
            else:
                outward[j] = lax.ppermute(both, "cell", HALF_LINE)
        elif kind == "gram":
            part, got1, got2, got3 = after(token, own[0], inward[0], across[0], outward[0])
            lanes = slice(tile - SPARE, tile - SPARE + columns)
            share = part[:, lanes] + jnp.where(
                inner, got1[:, lanes] + got2[:, lanes], got3[:, lanes]
            )
            packed = rows // 8
            share = jnp.concatenate(
                [share[i * packed : (i + 1) * packed] for i in range(8)], axis=1
            )
            pair = jnp.concatenate([share, swap(share, "gene", 1, 4)], axis=0)
            pair_got = swap(pair, "gene", 2, 4)
            token = pair
        elif kind == "gram_total":
            pair, pair_got = after(token, pair, pair_got)
            gram_left, gram_own = call(
                gram_total_kernel,
                (place, dataset_sizes),
                (pair, pair_got),
                [whole((2 * packed, 8 * columns))] * 2,
                [struct(rows, 3 * rank, dtype=bf16), struct(flat, tile)],
                [whole((rows, 3 * rank)), whole((flat, tile))],
                cost=cost(1000000, 200000),
            )
            token = gram_own
        elif kind == "sum":
            token = sum_step(j, token)
        elif kind == "factor":
            number = 2 if j == 0 else 1
            for k in range(j, j + number):
                if sums[k] is None:
                    sum_step(k, token)
            new_factors, token = factor_step(j, number, token, new_factors)
            if j == 0:
                grams = [value[2 * rank :, :tile] for value in totals[0]]
        else:
            new_shared = shared_step(j, 2 if j == 0 else 1, token, new_shared)
            token = new_shared
    return usage, new_factors, new_shared


def solution(mesh):
    sizes = (mesh.shape["dp"], mesh.shape["cell"], mesh.shape["gene"])
    return jax.shard_map(
        fast_body if sizes == (2, 4, 4) else plain_body,
        mesh=mesh,
        in_specs=(
            P("gene", ("dp", "cell")),
            P(None, ("dp", "cell")),
            P(None, "gene"),
            P("dp", None, "gene"),
            P(("dp", "cell")),
            P("dp"),
        ),
        out_specs=(P(None, ("dp", "cell")), P("dp", None, "gene"), P(None, "gene")),
        check_vma=False,
    )
```

```python
import functools

import jax
import jax.numpy as jnp
from jax import lax
from jax.experimental import pallas as pl
from jax.experimental.pallas import tpu as pltpu
from jax.sharding import PartitionSpec as P

ITERS = 3
penalty = 5.0
precise = lax.Precision.HIGHEST
f32 = jnp.float32
bf16 = jnp.bfloat16

GENE_TILE = 256
SPARE = 24
VMEM = pl.BlockSpec(memory_space=pltpu.VMEM)


def shared_update(shared_now, total_cross, total_gram, total_pull):
    for sweep in range(ITERS):
        shared_now = (
            shared_now
            * total_cross
            / (jnp.dot(total_gram, shared_now, precision=precise) + total_pull)
        )
    return shared_now


def plain_body(expression, usage_init, shared_factor, dataset_factors, cell_dataset, dataset_sizes):
    dataset_count = dataset_factors.shape[0]
    factor_rank = shared_factor.shape[0]
    gene_count = shared_factor.shape[1]
    slot_count = expression.shape[1]
    counted = dataset_sizes.astype(f32)
    onehot = (cell_dataset[None, :] == jnp.arange(dataset_count, dtype=jnp.int32)[:, None]).astype(f32)
    alive_mask = cell_dataset < dataset_count
    stacked_low = jnp.concatenate([shared_factor[None], dataset_factors], axis=0).astype(bf16)
    products = jnp.dot(
        stacked_low.reshape((dataset_count + 1) * factor_rank, gene_count),
        expression,
        preferred_element_type=f32,
    ).reshape(dataset_count + 1, factor_rank, slot_count)
    cross_part = products[0] + jnp.sum(onehot[:, None, :] * products[1:], axis=0)
    combined = shared_factor[None] + dataset_factors
    gram_part = jnp.einsum(
        "dkg,dlg->dkl", combined, combined, precision=precise
    ) + penalty * jnp.einsum("dkg,dlg->dkl", dataset_factors, dataset_factors, precision=precise)
    cross_sum, gram_full = lax.psum((cross_part, gram_part), "gene")
    usage_now = usage_init
    for sweep in range(ITERS):
        stacked = jnp.dot(
            gram_full.reshape(dataset_count * factor_rank, factor_rank),
            usage_now,
            precision=precise,
        ).reshape(dataset_count, factor_rank, slot_count)
        divisor = jnp.sum(onehot[:, None, :] * stacked, axis=0)
        divisor = jnp.where(alive_mask[None, :], divisor, 1.0)
        usage_now = jnp.where(alive_mask[None, :], usage_now * cross_sum / divisor, usage_now)
    masked_usage = onehot[:, None, :] * usage_now[None]
    low_usage = masked_usage.astype(bf16).reshape(dataset_count * factor_rank, slot_count)
    cross_stat_part = lax.dot_general(
        low_usage, expression, (((1,), (1,)), ((), ())), preferred_element_type=f32
    ).reshape(dataset_count, factor_rank, gene_count)
    cross_stat_part = cross_stat_part / counted[:, None, None]
    gram_stat_part = (
        jnp.einsum("dkc,dlc->dkl", masked_usage, masked_usage, precision=precise)
        / counted[:, None, None]
    )
    stat_cross, stat_gram = lax.psum((cross_stat_part, gram_stat_part), "cell")
    total_cross = jnp.sum(stat_cross, axis=0)
    total_gram = jnp.sum(stat_gram, axis=0)
    factor_now = dataset_factors
    for sweep in range(ITERS):
        divisor = jnp.einsum("dkl,lg->dkg", stat_gram, shared_factor, precision=precise) + (
            1.0 + penalty
        ) * jnp.einsum("dkl,dlg->dkg", stat_gram, factor_now, precision=precise)
        factor_now = factor_now * stat_cross / divisor
    total_pull = jnp.einsum("dkl,dlg->kg", stat_gram, factor_now, precision=precise)
    total_cross, total_gram, total_pull = lax.psum((total_cross, total_gram, total_pull), "dp")
    shared_now = shared_update(shared_factor, total_cross, total_gram, total_pull)
    return (usage_now, factor_now, shared_now)


def halves(value):
    high = value.astype(bf16)
    low = (value - high.astype(f32)).astype(bf16)
    return high, low


def nt_dot(a, b):
    return lax.dot_general(a, b, (((1,), (1,)), ((), ())), preferred_element_type=f32)


def left_cat(matrix):
    high, low = halves(matrix)
    return jnp.concatenate([high, low, high], axis=1)


def right_cat(value):
    high, low = halves(value)
    return jnp.concatenate([high, high, low], axis=0)


def thirds(value):
    high, rest = value.astype(bf16), value
    rest = rest - high.astype(f32)
    middle = rest.astype(bf16)
    low = (rest - middle.astype(f32)).astype(bf16)
    return high, middle, low


def fine_left(matrix):
    high, middle, low = thirds(matrix)
    return jnp.concatenate([high, high, middle, middle, high, low], axis=1)


def fine_right(value):
    high, middle, low = thirds(value)
    return jnp.concatenate([high, middle, high, middle, low, high], axis=0)


def flatten(block, width):
    parts = width // block.shape[1]
    rows = block.shape[0] // parts
    return jnp.concatenate([block[i * rows : (i + 1) * rows] for i in range(parts)], axis=1)


def unflatten(flat, rank):
    parts = flat.shape[1] // rank
    return jnp.concatenate([flat[:, i * rank : (i + 1) * rank] for i in range(parts)], axis=0)


def start_kernel(
    index_ref, shared_hbm, factors_hbm, expression_hbm, label_ref, send_ref, keep_ref,
    shared_ref, factors_ref, tile_ref, low_ref, sems,
):
    count, rank, genes = factors_ref.shape
    tiles, _, width = tile_ref.shape
    core = index_ref[0]

    def first_cell(t):
        which = jnp.where(t < tiles // 2, 1 - core, core) * (tiles // 2) + t % (tiles // 2)
        return pl.multiple_of(which * width, width)

    def tile_copy(t):
        return pltpu.make_async_copy(
            expression_hbm.at[:, pl.ds(first_cell(t), width)], tile_ref.at[t], sems.at[1 + count + t]
        )

    def factor_copy(e):
        return pltpu.make_async_copy(factors_hbm.at[e], factors_ref.at[e], sems.at[1 + e])

    shared_copy = pltpu.make_async_copy(shared_hbm, shared_ref, sems.at[0])
    shared_copy.start()
    for e in range(count):
        factor_copy(e).start()
    tile_copy(0).start()
    shared_copy.wait()
    for e in range(count):
        factor_copy(e).wait()
    for t in range(1, tiles):
        tile_copy(t).start()
    shared = shared_ref[...]
    shared_high, shared_low = halves(shared)
    low_ref[:rank, :] = shared_high
    pair = nt_dot(shared_high, jnp.concatenate([shared_high, shared_low], axis=0))
    shared_gram = pair[:, :rank] + pair[:, rank:] + pair[:, rank:].T
    out_width = send_ref.shape[1]
    rows = rank * rank // out_width
    for e in range(count):
        own = factors_ref[e]
        own_high, own_low = halves(own)
        low_ref[(e + 1) * rank : (e + 2) * rank, :] = own_high
        result = nt_dot(
            jnp.concatenate([shared_high, own_high], axis=0),
            jnp.concatenate([own_high, own_low, shared_low], axis=0),
        )
        cross = result[:rank, :rank] + result[:rank, rank : 2 * rank] + result[rank:, 2 * rank :].T
        mixed = cross + (1.0 + penalty) * result[rank:, rank : 2 * rank]
        block = shared_gram + (1.0 + penalty) * result[rank:, :rank]
        flat = flatten(block + mixed + mixed.T, out_width)
        send_ref[rank + e * rows : rank + (e + 1) * rows, :] = flat
        keep_ref[rank + e * rows : rank + (e + 1) * rows, :] = flat

    for t in range(tiles):
        tile_copy(t).wait()
        products = jnp.dot(low_ref[...], tile_ref[t], preferred_element_type=f32)
        label = label_ref[:, pl.ds(first_cell(t), width)]
        total = products[:rank]
        for e in range(count):
            total += jnp.where(label == e, products[(e + 1) * rank : (e + 2) * rank], 0.0)
        out = send_ref if t < tiles // 2 else keep_ref
        at = t % (tiles // 2) * width
        out[:rank, at : at + width] = total


def usage_kernel(index_ref, own_ref, other_ref, usage_ref, label_ref, out_ref):
    rank = usage_ref.shape[0]
    both = own_ref[...] + other_ref[...]
    cross = both[:rank]
    rows = rank * rank // both.shape[1]
    count = both.shape[0] // rows - rank // rows
    left = fine_left(
        jnp.concatenate(
            [unflatten(both[rank + e * rows : rank + (e + 1) * rows], rank) for e in range(count)],
            axis=0,
        )
    )
    label = label_ref[...]
    alive = label < count
    usage = usage_ref[...]
    for sweep in range(ITERS):
        stacked = jnp.dot(left, fine_right(usage), preferred_element_type=f32)
        divisor = jnp.where(alive, 0.0, 1.0)
        for e in range(count):
            divisor += jnp.where(label == e, stacked[e * rank : (e + 1) * rank], 0.0)
        usage = jnp.where(alive, usage * cross / divisor, usage)
    out_ref[...] = usage


def half_statistics(usage, label, expression, low_ref):
    rank, half = usage.shape
    count = low_ref.shape[0] // rank
    high, low = halves(usage)
    right = jnp.concatenate([high, low], axis=0)
    grams = []
    for e in range(count):
        masked = jnp.where(label == e, high, jnp.zeros_like(high))
        low_ref[e * rank : (e + 1) * rank, :] = masked
        grams.append(nt_dot(masked, right))
    return nt_dot(low_ref[...], expression), grams


def own_half_kernel(index_ref, own_ref, label_ref, expression_ref, low_ref, part_ref, gram_ref):
    rank = own_ref.shape[0]
    part, grams = half_statistics(own_ref[...], label_ref[...], expression_ref[...], low_ref)
    part_ref[...] = part
    for e, gram in enumerate(grams):
        gram_ref[e * rank : (e + 1) * rank, :] = gram


def first_stat_kernel(
    index_ref, place_ref, other_ref, own_part_ref, own_gram_ref, label_ref, expression_ref,
    low_ref, part_ref,
):
    rank, half = other_ref.shape
    count = low_ref.shape[0] // rank
    part, grams = half_statistics(other_ref[...], label_ref[...], expression_ref[...], low_ref)
    part_ref[...] = part + own_part_ref[...]
    columns = rank // 4
    for e in range(count):
        rows = slice(e * rank, (e + 1) * rank)
        both = grams[e] + own_gram_ref[rows, :]
        mixed = both[:, rank:]
        gram = both[:, :rank] + mixed + mixed.T
        share = gram[:, :columns]
        for k in range(1, rank // columns):
            share = jnp.where(place_ref[0] == k, gram[:, k * columns : (k + 1) * columns], share)
        part_ref[rows, -SPARE : columns - SPARE] = share


def stat_kernel(
    index_ref, own_ref, other_ref, low_ref, other_low_ref, expression_ref, other_expression_ref,
    usage_ref, *parts,
):
    step = pl.program_id(0)
    half = own_ref.shape[1]

    @pl.when(step == 0)
    def _():
        core = index_ref[0]
        usage_ref[:, pl.ds(pl.multiple_of(core * half, half), half)] = own_ref[...]
        usage_ref[:, pl.ds(pl.multiple_of((1 - core) * half, half), half)] = other_ref[...]

    result = nt_dot(low_ref[...], expression_ref[...])
    result += nt_dot(other_low_ref[...], other_expression_ref[...])
    for t, ref in enumerate(parts):
        @pl.when(step == t)
        def _():
            ref[...] = result


def gram_total_kernel(place_ref, size_ref, pair_ref, other_ref, left_ref, total_ref):
    width = total_ref.shape[1]
    rank = left_ref.shape[1] // 3
    count = left_ref.shape[0] // rank
    columns = pair_ref.shape[1] // 8
    packed = pair_ref.shape[0] // 2
    place = place_ref[0]
    shares = [
        jnp.concatenate(
            [
                ref[at : at + packed, i * columns : (i + 1) * columns]
                for i in range(8)
            ],
            axis=0,
        )
        for ref in (pair_ref, other_ref)
        for at in (0, packed)
    ]
    whole_gram = []
    for k in range(rank // columns):
        share = shares[0]
        for offset in range(1, rank // columns):
            share = jnp.where(place == k ^ offset, shares[offset], share)
        whole_gram.append(share)
    gram = jnp.concatenate(whole_gram, axis=1)
    total = jnp.zeros((rank, rank), f32)
    for e in range(count):
        rows = slice(e * rank, (e + 1) * rank)
        scaled = gram[rows] / size_ref[e].astype(f32)
        left_ref[rows, :] = left_cat(scaled)
        total += scaled
    total_ref[...] = flatten(total, width)


def factor_kernel(tiles, size_ref, *refs):
    crosses_ref, (left_ref, gram_ref, shared_ref, factors_ref) = refs[:tiles], refs[tiles : tiles + 4]
    out_ref, total_ref = refs[-2:]
    count, rank, width = factors_ref.shape
    shared = shared_ref[...]
    lefts = [left_ref[e * rank : (e + 1) * rank, :] for e in range(count)]
    crosses = [
        jnp.concatenate([ref[e * rank : (e + 1) * rank, :] for ref in crosses_ref], axis=1)
        * (1.0 / size_ref[e].astype(f32))
        for e in range(count)
    ]
    factors = [factors_ref[e] for e in range(count)]
    for sweep in range(ITERS):
        divisors = [
            jnp.dot(
                lefts[e],
                right_cat(shared + (1.0 + penalty) * factors[e]),
                preferred_element_type=f32,
            )
            for e in range(count)
        ]
        factors = [factors[e] * crosses[e] / divisors[e] for e in range(count)]
    total_cross = jnp.zeros((rank, width), f32)
    total_pull = jnp.zeros((rank, width), f32)
    for e in range(count):
        out_ref[e] = factors[e]
        total_cross += crosses[e]
        total_pull += jnp.dot(lefts[e], right_cat(factors[e]), preferred_element_type=f32)
    total_ref[:rank, :] = total_cross
    total_ref[rank : 2 * rank, :] = total_pull
    if total_ref.shape[0] > 2 * rank:
        total_ref[2 * rank :, : gram_ref.shape[1]] = gram_ref[...]
        total_ref[2 * rank :, gram_ref.shape[1] :] = jnp.zeros_like(gram_ref)


def shared_kernel(own_ref, other_ref, gram_own, gram_other, shared_ref, *rest):
    out_ref = rest[-1]
    rank = out_ref.shape[0]
    total = own_ref[...] + other_ref[...]
    left = left_cat(unflatten(gram_own[...] + gram_other[...], rank))
    shared = shared_ref[...]
    for sweep in range(ITERS):
        divisor = jnp.dot(left, right_cat(shared), preferred_element_type=f32) + total[rank : 2 * rank]
        shared = shared * total[:rank] / divisor
    out_ref[...] = shared


def struct(*shape, dtype=f32):
    return jax.ShapeDtypeStruct(shape, dtype)


def whole(shape):
    return pl.BlockSpec(shape, lambda *_: (0,) * len(shape))


def call(
    kernel, index, args, in_specs, out_shape, out_specs,
    grid=(1,), scratch=(), cost=None, aliases={}, vmem=16,
):
    return pl.pallas_call(
        kernel,
        grid_spec=pltpu.PrefetchScalarGridSpec(
            num_scalar_prefetch=len(index),
            grid=grid,
            in_specs=in_specs,
            out_specs=out_specs,
            scratch_shapes=list(scratch),
        ),
        out_shape=out_shape,
        compiler_params=pltpu.CompilerParams(vmem_limit_bytes=int(vmem * 1024 * 1024)),
        cost_estimate=cost,
        input_output_aliases=aliases,
    )(*index, *args)


def cost(flops, moved):
    return pl.CostEstimate(flops=int(flops), bytes_accessed=int(moved), transcendentals=0)


def swap(value, axis, offset, size):
    return lax.ppermute(value, axis, [(i, i ^ offset) for i in range(size)])


HALF_LINE = [(0, 1), (1, 0), (2, 3), (3, 2)]
ACROSS = [(4 * g + c, 4 * g + 3 - c) for g in (0, 1) for c in (1, 2)] + [
    (4 * g + c, 4 * (1 - g) + c) for g in (0, 1) for c in (0, 3)
]


ORDER = (
    ("across", 0),
    ("across", 1),
    ("outward", 0),
    ("across", 2),
    ("outward", 1),
    ("across", 3),
    ("gram", 0),
    ("outward", 2),
    ("sum", 1),
    ("gram_total", 0),
    ("factor", 0),
    ("outward", 3),
    ("factor", 2),
    ("factor", 3),
    ("shared", 0),
    ("shared", 2),
    ("shared", 3),
)


def fast_body(expression, usage_init, shared_factor, dataset_factors, cell_dataset, dataset_sizes):
    count, rank, genes = dataset_factors.shape
    cells = expression.shape[1]
    half = cells // 2
    tile = GENE_TILE
    core = lax.axis_index("gene") % 2
    index = core.astype(jnp.int32).reshape(1)
    place = lax.axis_index("gene").astype(jnp.int32).reshape(1)
    label = cell_dataset.reshape(1, cells)
    rows = count * rank
    flat = rank * rank // tile

    hbm = pl.BlockSpec(memory_space=pltpu.HBM)
    cell_tile = 512
    shape = (rank + count * rank * rank // half, half)
    send, keep = call(
        start_kernel,
        (index,),
        (shared_factor, dataset_factors, expression, label),
        [hbm, hbm, hbm, whole((1, cells))],
        [struct(*shape), struct(*shape)],
        [whole(shape), whole(shape)],
        scratch=[
            pltpu.VMEM((rank, genes), f32),
            pltpu.VMEM((count, rank, genes), f32),
            pltpu.VMEM((cells // cell_tile, genes, cell_tile), bf16),
            pltpu.VMEM((rows + rank, genes), bf16),
            pltpu.SemaphoreType.DMA((1 + count + cells // cell_tile,)),
        ],
        vmem=53.5,
        cost=cost(2 * (count + 1) * rank * genes * cells, 2 * genes * cells),
    )
    both = keep + swap(send, "gene", 1, 4)
    both_more = swap(both, "gene", 2, 4)
    usage_half = call(
        usage_kernel,
        (index,),
        (both, both_more, usage_init, label),
        [
            whole(shape),
            whole(shape),
            pl.BlockSpec((rank, half), lambda i, idx: (0, idx[0])),
            pl.BlockSpec((1, half), lambda i, idx: (0, idx[0])),
        ],
        struct(rank, half),
        whole((rank, half)),
        cost=cost(2 * ITERS * 3 * count * rank * rank * half, 16 * rank * half),
    )
    usage_other = swap(usage_half, "gene", 1, 4)

    pieces = pl.cdiv(genes, tile)
    columns = rank // 4
    low_half, part_half, gram_half = call(
        own_half_kernel,
        (index,),
        (usage_half, label, expression),
        [
            whole((rank, half)),
            pl.BlockSpec((1, half), lambda i, idx: (0, idx[0])),
            pl.BlockSpec((tile, half), lambda i, idx: (pieces - 1, idx[0])),
        ],
        [struct(rows, half, dtype=bf16), struct(rows, tile), struct(rows, 2 * rank)],
        [whole((rows, half)), whole((rows, tile)), whole((rows, 2 * rank))],
        cost=cost(2 * rows * (tile + 2 * rank) * half, 2 * tile * half),
    )
    other_low, first = call(
        first_stat_kernel,
        (index, place),
        (usage_other, part_half, gram_half, label, expression),
        [
            whole((rank, half)),
            whole((rows, tile)),
            whole((rows, 2 * rank)),
            pl.BlockSpec((1, half), lambda i, idx, _: (0, 1 - idx[0])),
            pl.BlockSpec((tile, half), lambda i, idx, _: (pieces - 1, 1 - idx[0])),
        ],
        [struct(rows, half, dtype=bf16), struct(rows, tile)],
        [whole((rows, half)), whole((rows, tile))],
        cost=cost(2 * rows * (tile + 2 * rank) * half, 2 * tile * half),
    )
    usage, *others = call(
        stat_kernel,
        (index,),
        (usage_half, usage_other, low_half, other_low, expression, expression),
        [
            whole((rank, half)),
            whole((rank, half)),
            whole((rows, half)),
            whole((rows, half)),
            pl.BlockSpec((tile, half), lambda i, idx: (pieces - 2 - i, idx[0])),
            pl.BlockSpec((tile, half), lambda i, idx: (pieces - 2 - i, 1 - idx[0])),
        ],
        [struct(rank, cells)] + [struct(rows, tile)] * (pieces - 1),
        [whole((rank, cells))] + [whole((rows, tile))] * (pieces - 1),
        grid=(pieces - 1,),
        cost=cost(2 * rows * genes * cells, 2 * genes * cells),
    )
    own = [first] + others

    depth = lax.axis_index("cell")
    inner = (depth == 1) | (depth == 2)
    last = pieces - 1
    inward = [lax.ppermute(part, "cell", HALF_LINE) for part in own[:last]] + [None]
    across = [None] * pieces
    outward = [None] * pieces
    totals = [None] * pieces
    token = own[1]

    def after(token, *values):
        *values, token = lax.optimization_barrier((*values, token))
        return values

    new_factors = None
    new_shared = None
    gram_left = None
    grams = None
    gram_own = None

    def shared_call(block_at, width, own_total, other_total, into):
        shape = (2 * rank, width)
        block = pl.BlockSpec((rank, width), lambda i: (0, block_at))
        more = () if into is None else (into,)
        return call(
            shared_kernel,
            (),
            (own_total, other_total, *grams, shared_factor) + more,
            [whole(shape)] * 2
            + [whole((flat, tile))] * 2
            + [block]
            + [pl.BlockSpec(memory_space=pl.ANY)] * len(more),
            struct(rank, genes),
            block,
            aliases={5: 0} if more else {},
            cost=cost(2 * 3 * 3 * rank * rank * width, 6 * 4 * rank * width),
        )

    sums = [None] * pieces

    def sum_step(j, token):
        part, got1, got2, got3 = after(token, own[j], inward[j], across[j], outward[j])
        sums[j] = part + jnp.where(inner, got1 + got2, got3)
        return sums[j]

    def factor_step(first, number, token, into):
        width = number * tile
        block_at = (pieces - first - number) // number
        gene_block = pl.BlockSpec((rank, width), lambda i, idx: (0, block_at))
        set_block = pl.BlockSpec((count, rank, width), lambda i, idx: (0, 0, block_at))
        more = () if into is None else (into,)
        shape = (2 * rank + (flat if first == 0 else 0), width)
        *crosses, _ = lax.optimization_barrier((*sums[first : first + number][::-1], token))
        into, own_total = call(
            functools.partial(factor_kernel, number),
            (dataset_sizes,),
            (*crosses, gram_left, gram_own, shared_factor, dataset_factors) + more,
            [whole((rows, tile))] * number
            + [whole((rows, 3 * rank)), whole((flat, tile)), gene_block, set_block]
            + [pl.BlockSpec(memory_space=pl.ANY)] * len(more),
            [struct(count, rank, genes), struct(*shape)],
            [set_block, whole(shape)],
            aliases={5 + number: 0} if more else {},
            cost=cost(2 * 4 * 3 * rows * rank * width, 3 * 4 * rows * width),
        )
        totals[first] = (own_total, swap(own_total, "dp", 1, 2))
        return into, own_total

    def shared_step(first, number, token, into):
        own_total, other_total = after(token, *totals[first])
        return shared_call(
            (pieces - first - number) // number,
            number * tile,
            own_total[: 2 * rank],
            other_total[: 2 * rank],
            into,
        )

    for step in ORDER:
        kind, j = step
        if kind == "across":
            part, got = after(token, own[j], inward[j])
            both = part + got
            across[j] = lax.ppermute(both, ("dp", "cell"), ACROSS)
            token = both if j == 2 else got
        elif kind == "outward":
            part, got = after(token, own[j], across[j])
            both, token = part + got, got
            if j == 0:
                mixed = jnp.where(inner, both, own[last])
                inward[last] = outward[0] = lax.ppermute(mixed, "cell", HALF_LINE)
            else:
                outward[j] = lax.ppermute(both, "cell", HALF_LINE)
        elif kind == "gram":
            share = sum_step(0, token)[:, tile - SPARE : tile - SPARE + columns]
            packed = rows // 8
            share = jnp.concatenate(
                [share[i * packed : (i + 1) * packed] for i in range(8)], axis=1
            )
            pair = jnp.concatenate([share, swap(share, "gene", 1, 4)], axis=0)
            pair_got = swap(pair, "gene", 2, 4)
            token = pair
        elif kind == "gram_total":
            pair, pair_got = after(token, pair, pair_got)
            gram_left, gram_own = call(
                gram_total_kernel,
                (place, dataset_sizes),
                (pair, pair_got),
                [whole((2 * packed, 8 * columns))] * 2,
                [struct(rows, 3 * rank, dtype=bf16), struct(flat, tile)],
                [whole((rows, 3 * rank)), whole((flat, tile))],
                cost=cost(1000000, 200000),
            )
            token = gram_own
        elif kind == "sum":
            token = sum_step(j, token)
        elif kind == "factor":
            number = 2 if j == 0 else 1
            for k in range(j, j + number):
                if sums[k] is None:
                    sum_step(k, token)
            new_factors, token = factor_step(j, number, token, new_factors)
            if j == 0:
                grams = [value[2 * rank :, :tile] for value in totals[0]]
        else:
            new_shared = shared_step(j, 2 if j == 0 else 1, token, new_shared)
            token = new_shared
    return usage, new_factors, new_shared


def solution(mesh):
    sizes = (mesh.shape["dp"], mesh.shape["cell"], mesh.shape["gene"])
    return jax.shard_map(
        fast_body if sizes == (2, 4, 4) else plain_body,
        mesh=mesh,
        in_specs=(
            P("gene", ("dp", "cell")),
            P(None, ("dp", "cell")),
            P(None, "gene"),
            P("dp", None, "gene"),
            P(("dp", "cell")),
            P("dp"),
        ),
        out_specs=(P(None, ("dp", "cell")), P("dp", None, "gene"), P(None, "gene")),
        check_vma=False,
    )
```

```python
import functools

import jax
import jax.numpy as jnp
from jax import lax
from jax.experimental import pallas as pl
from jax.experimental.pallas import tpu as pltpu
from jax.sharding import PartitionSpec as P

ITERS = 3
penalty = 5.0
precise = lax.Precision.HIGHEST
f32 = jnp.float32
bf16 = jnp.bfloat16

GENE_TILE = 256
SPARE = 24
VMEM = pl.BlockSpec(memory_space=pltpu.VMEM)


def shared_update(shared_now, total_cross, total_gram, total_pull):
    for sweep in range(ITERS):
        shared_now = (
            shared_now
            * total_cross
            / (jnp.dot(total_gram, shared_now, precision=precise) + total_pull)
        )
    return shared_now


def plain_body(expression, usage_init, shared_factor, dataset_factors, cell_dataset, dataset_sizes):
    dataset_count = dataset_factors.shape[0]
    factor_rank = shared_factor.shape[0]
    gene_count = shared_factor.shape[1]
    slot_count = expression.shape[1]
    counted = dataset_sizes.astype(f32)
    onehot = (cell_dataset[None, :] == jnp.arange(dataset_count, dtype=jnp.int32)[:, None]).astype(f32)
    alive_mask = cell_dataset < dataset_count
    stacked_low = jnp.concatenate([shared_factor[None], dataset_factors], axis=0).astype(bf16)
    products = jnp.dot(
        stacked_low.reshape((dataset_count + 1) * factor_rank, gene_count),
        expression,
        preferred_element_type=f32,
    ).reshape(dataset_count + 1, factor_rank, slot_count)
    cross_part = products[0] + jnp.sum(onehot[:, None, :] * products[1:], axis=0)
    combined = shared_factor[None] + dataset_factors
    gram_part = jnp.einsum(
        "dkg,dlg->dkl", combined, combined, precision=precise
    ) + penalty * jnp.einsum("dkg,dlg->dkl", dataset_factors, dataset_factors, precision=precise)
    cross_sum, gram_full = lax.psum((cross_part, gram_part), "gene")
    usage_now = usage_init
    for sweep in range(ITERS):
        stacked = jnp.dot(
            gram_full.reshape(dataset_count * factor_rank, factor_rank),
            usage_now,
            precision=precise,
        ).reshape(dataset_count, factor_rank, slot_count)
        divisor = jnp.sum(onehot[:, None, :] * stacked, axis=0)
        divisor = jnp.where(alive_mask[None, :], divisor, 1.0)
        usage_now = jnp.where(alive_mask[None, :], usage_now * cross_sum / divisor, usage_now)
    masked_usage = onehot[:, None, :] * usage_now[None]
    low_usage = masked_usage.astype(bf16).reshape(dataset_count * factor_rank, slot_count)
    cross_stat_part = lax.dot_general(
        low_usage, expression, (((1,), (1,)), ((), ())), preferred_element_type=f32
    ).reshape(dataset_count, factor_rank, gene_count)
    cross_stat_part = cross_stat_part / counted[:, None, None]
    gram_stat_part = (
        jnp.einsum("dkc,dlc->dkl", masked_usage, masked_usage, precision=precise)
        / counted[:, None, None]
    )
    stat_cross, stat_gram = lax.psum((cross_stat_part, gram_stat_part), "cell")
    total_cross = jnp.sum(stat_cross, axis=0)
    total_gram = jnp.sum(stat_gram, axis=0)
    factor_now = dataset_factors
    for sweep in range(ITERS):
        divisor = jnp.einsum("dkl,lg->dkg", stat_gram, shared_factor, precision=precise) + (
            1.0 + penalty
        ) * jnp.einsum("dkl,dlg->dkg", stat_gram, factor_now, precision=precise)
        factor_now = factor_now * stat_cross / divisor
    total_pull = jnp.einsum("dkl,dlg->kg", stat_gram, factor_now, precision=precise)
    total_cross, total_gram, total_pull = lax.psum((total_cross, total_gram, total_pull), "dp")
    shared_now = shared_update(shared_factor, total_cross, total_gram, total_pull)
    return (usage_now, factor_now, shared_now)


def halves(value):
    high = value.astype(bf16)
    low = (value - high.astype(f32)).astype(bf16)
    return high, low


def nt_dot(a, b):
    return lax.dot_general(a, b, (((1,), (1,)), ((), ())), preferred_element_type=f32)


def left_cat(matrix):
    high, low = halves(matrix)
    return jnp.concatenate([high, low, high], axis=1)


def right_cat(value):
    high, low = halves(value)
    return jnp.concatenate([high, high, low], axis=0)


def thirds(value):
    high, rest = value.astype(bf16), value
    rest = rest - high.astype(f32)
    middle = rest.astype(bf16)
    low = (rest - middle.astype(f32)).astype(bf16)
    return high, middle, low


def fine_left(matrix):
    high, middle, low = thirds(matrix)
    return jnp.concatenate([high, high, middle, middle, high, low], axis=1)


def fine_right(value):
    high, middle, low = thirds(value)
    return jnp.concatenate([high, middle, high, middle, low, high], axis=0)


def flatten(block, width):
    parts = width // block.shape[1]
    rows = block.shape[0] // parts
    return jnp.concatenate([block[i * rows : (i + 1) * rows] for i in range(parts)], axis=1)


def unflatten(flat, rank):
    parts = flat.shape[1] // rank
    return jnp.concatenate([flat[:, i * rank : (i + 1) * rank] for i in range(parts)], axis=0)


def start_kernel(
    index_ref, shared_hbm, factors_hbm, expression_hbm, label_ref, send_ref, keep_ref,
    shared_ref, factors_ref, tile_ref, low_ref, sems,
):
    count, rank, genes = factors_ref.shape
    tiles, _, width = tile_ref.shape
    core = index_ref[0]

    def first_cell(t):
        which = jnp.where(t < tiles // 2, 1 - core, core) * (tiles // 2) + t % (tiles // 2)
        return pl.multiple_of(which * width, width)

    def tile_copy(t):
        return pltpu.make_async_copy(
            expression_hbm.at[:, pl.ds(first_cell(t), width)], tile_ref.at[t], sems.at[1 + count + t]
        )

    def factor_copy(e):
        return pltpu.make_async_copy(factors_hbm.at[e], factors_ref.at[e], sems.at[1 + e])

    shared_copy = pltpu.make_async_copy(shared_hbm, shared_ref, sems.at[0])
    shared_copy.start()
    for e in range(count):
        factor_copy(e).start()
    tile_copy(0).start()
    shared_copy.wait()
    for e in range(count):
        factor_copy(e).wait()
    for t in range(1, tiles):
        tile_copy(t).start()
    shared = shared_ref[...]
    shared_high, shared_low = halves(shared)
    low_ref[:rank, :] = shared_high
    pair = nt_dot(shared_high, jnp.concatenate([shared_high, shared_low], axis=0))
    shared_gram = pair[:, :rank] + pair[:, rank:] + pair[:, rank:].T
    out_width = send_ref.shape[1]
    rows = rank * rank // out_width
    for e in range(count):
        own = factors_ref[e]
        own_high, own_low = halves(own)
        low_ref[(e + 1) * rank : (e + 2) * rank, :] = own_high
        result = nt_dot(
            jnp.concatenate([shared_high, own_high], axis=0),
            jnp.concatenate([own_high, own_low, shared_low], axis=0),
        )
        cross = result[:rank, :rank] + result[:rank, rank : 2 * rank] + result[rank:, 2 * rank :].T
        mixed = cross + (1.0 + penalty) * result[rank:, rank : 2 * rank]
        block = shared_gram + (1.0 + penalty) * result[rank:, :rank]
        flat = flatten(block + mixed + mixed.T, out_width)
        send_ref[rank + e * rows : rank + (e + 1) * rows, :] = flat
        keep_ref[rank + e * rows : rank + (e + 1) * rows, :] = flat

    for t in range(tiles):
        tile_copy(t).wait()
        products = jnp.dot(low_ref[...], tile_ref[t], preferred_element_type=f32)
        label = label_ref[:, pl.ds(first_cell(t), width)]
        total = products[:rank]
        for e in range(count):
            total += jnp.where(label == e, products[(e + 1) * rank : (e + 2) * rank], 0.0)
        out = send_ref if t < tiles // 2 else keep_ref
        at = t % (tiles // 2) * width
        out[:rank, at : at + width] = total


def usage_kernel(index_ref, own_ref, other_ref, usage_ref, label_ref, out_ref):
    rank = usage_ref.shape[0]
    both = own_ref[...] + other_ref[...]
    cross = both[:rank]
    rows = rank * rank // both.shape[1]
    count = both.shape[0] // rows - rank // rows
    left = fine_left(
        jnp.concatenate(
            [unflatten(both[rank + e * rows : rank + (e + 1) * rows], rank) for e in range(count)],
            axis=0,
        )
    )
    label = label_ref[...]
    alive = label < count
    usage = usage_ref[...]
    for sweep in range(ITERS):
        stacked = jnp.dot(left, fine_right(usage), preferred_element_type=f32)
        divisor = jnp.where(alive, 0.0, 1.0)
        for e in range(count):
            divisor += jnp.where(label == e, stacked[e * rank : (e + 1) * rank], 0.0)
        usage = jnp.where(alive, usage * cross / divisor, usage)
    out_ref[...] = usage


def half_statistics(usage, label, expression, low_ref):
    rank, half = usage.shape
    count = low_ref.shape[0] // rank
    high, low = halves(usage)
    right = jnp.concatenate([high, low], axis=0)
    grams = []
    for e in range(count):
        masked = jnp.where(label == e, high, jnp.zeros_like(high))
        low_ref[e * rank : (e + 1) * rank, :] = masked
        grams.append(nt_dot(masked, right))
    return nt_dot(low_ref[...], expression), grams


def own_half_kernel(index_ref, own_ref, label_ref, expression_ref, low_ref, part_ref, gram_ref):
    rank = own_ref.shape[0]
    part, grams = half_statistics(own_ref[...], label_ref[...], expression_ref[...], low_ref)
    part_ref[...] = part
    for e, gram in enumerate(grams):
        gram_ref[e * rank : (e + 1) * rank, :] = gram


def first_stat_kernel(
    index_ref, place_ref, other_ref, own_part_ref, own_gram_ref, label_ref, expression_ref,
    low_ref, part_ref,
):
    rank, half = other_ref.shape
    count = low_ref.shape[0] // rank
    part, grams = half_statistics(other_ref[...], label_ref[...], expression_ref[...], low_ref)
    part_ref[...] = part + own_part_ref[...]
    columns = rank // 4
    for e in range(count):
        rows = slice(e * rank, (e + 1) * rank)
        both = grams[e] + own_gram_ref[rows, :]
        mixed = both[:, rank:]
        gram = both[:, :rank] + mixed + mixed.T
        share = gram[:, :columns]
        for k in range(1, rank // columns):
            share = jnp.where(place_ref[0] == k, gram[:, k * columns : (k + 1) * columns], share)
        part_ref[rows, -SPARE : columns - SPARE] = share


def stat_kernel(
    index_ref, own_ref, other_ref, low_ref, other_low_ref, expression_ref, other_expression_ref,
    usage_ref, *parts,
):
    step = pl.program_id(0)
    half = own_ref.shape[1]

    @pl.when(step == 0)
    def _():
        core = index_ref[0]
        usage_ref[:, pl.ds(pl.multiple_of(core * half, half), half)] = own_ref[...]
        usage_ref[:, pl.ds(pl.multiple_of((1 - core) * half, half), half)] = other_ref[...]

    result = nt_dot(low_ref[...], expression_ref[...])
    result += nt_dot(other_low_ref[...], other_expression_ref[...])
    for t, ref in enumerate(parts):
        @pl.when(step == t)
        def _():
            ref[...] = result


def gram_total_kernel(place_ref, size_ref, pair_ref, other_ref, left_ref, total_ref):
    width = total_ref.shape[1]
    rank = left_ref.shape[1] // 3
    count = left_ref.shape[0] // rank
    columns = pair_ref.shape[1] // 8
    packed = pair_ref.shape[0] // 2
    place = place_ref[0]
    shares = [
        jnp.concatenate(
            [
                ref[at : at + packed, i * columns : (i + 1) * columns]
                for i in range(8)
            ],
            axis=0,
        )
        for ref in (pair_ref, other_ref)
        for at in (0, packed)
    ]
    whole_gram = []
    for k in range(rank // columns):
        share = shares[0]
        for offset in range(1, rank // columns):
            share = jnp.where(place == k ^ offset, shares[offset], share)
        whole_gram.append(share)
    gram = jnp.concatenate(whole_gram, axis=1)
    total = jnp.zeros((rank, rank), f32)
    for e in range(count):
        rows = slice(e * rank, (e + 1) * rank)
        scaled = gram[rows] / size_ref[e].astype(f32)
        left_ref[rows, :] = left_cat(scaled)
        total += scaled
    total_ref[...] = flatten(total, width)


def factor_kernel(tiles, size_ref, *refs):
    crosses_ref, (left_ref, gram_ref, shared_ref, factors_ref) = refs[:tiles], refs[tiles : tiles + 4]
    out_ref, total_ref = refs[-2:]
    count, rank, width = factors_ref.shape
    shared = shared_ref[...]
    lefts = [left_ref[e * rank : (e + 1) * rank, :] for e in range(count)]
    crosses = [
        jnp.concatenate([ref[e * rank : (e + 1) * rank, :] for ref in crosses_ref], axis=1)
        * (1.0 / size_ref[e].astype(f32))
        for e in range(count)
    ]
    factors = [factors_ref[e] for e in range(count)]
    for sweep in range(ITERS):
        divisors = [
            jnp.dot(
                lefts[e],
                right_cat(shared + (1.0 + penalty) * factors[e]),
                preferred_element_type=f32,
            )
            for e in range(count)
        ]
        factors = [factors[e] * crosses[e] / divisors[e] for e in range(count)]
    total_cross = jnp.zeros((rank, width), f32)
    total_pull = jnp.zeros((rank, width), f32)
    for e in range(count):
        out_ref[e] = factors[e]
        total_cross += crosses[e]
        total_pull += jnp.dot(lefts[e], right_cat(factors[e]), preferred_element_type=f32)
    total_ref[:rank, :] = total_cross
    total_ref[rank : 2 * rank, :] = total_pull
    if total_ref.shape[0] > 2 * rank:
        total_ref[2 * rank :, : gram_ref.shape[1]] = gram_ref[...]
        total_ref[2 * rank :, gram_ref.shape[1] :] = jnp.zeros_like(gram_ref)


def shared_kernel(own_ref, other_ref, gram_own, gram_other, shared_ref, *rest):
    out_ref = rest[-1]
    rank = out_ref.shape[0]
    total = own_ref[...] + other_ref[...]
    left = left_cat(unflatten(gram_own[...] + gram_other[...], rank))
    shared = shared_ref[...]
    for sweep in range(ITERS):
        divisor = jnp.dot(left, right_cat(shared), preferred_element_type=f32) + total[rank : 2 * rank]
        shared = shared * total[:rank] / divisor
    out_ref[...] = shared


def struct(*shape, dtype=f32):
    return jax.ShapeDtypeStruct(shape, dtype)


def whole(shape):
    return pl.BlockSpec(shape, lambda *_: (0,) * len(shape))


def call(
    kernel, index, args, in_specs, out_shape, out_specs,
    grid=(1,), scratch=(), cost=None, aliases={}, vmem=16,
):
    return pl.pallas_call(
        kernel,
        grid_spec=pltpu.PrefetchScalarGridSpec(
            num_scalar_prefetch=len(index),
            grid=grid,
            in_specs=in_specs,
            out_specs=out_specs,
            scratch_shapes=list(scratch),
        ),
        out_shape=out_shape,
        compiler_params=pltpu.CompilerParams(vmem_limit_bytes=int(vmem * 1024 * 1024)),
        cost_estimate=cost,
        input_output_aliases=aliases,
    )(*index, *args)


def cost(flops, moved):
    return pl.CostEstimate(flops=int(flops), bytes_accessed=int(moved), transcendentals=0)


def swap(value, axis, offset, size):
    return lax.ppermute(value, axis, [(i, i ^ offset) for i in range(size)])


HALF_LINE = [(0, 1), (1, 0), (2, 3), (3, 2)]
ACROSS = [(4 * g + c, 4 * g + 3 - c) for g in (0, 1) for c in (1, 2)] + [
    (4 * g + c, 4 * (1 - g) + c) for g in (0, 1) for c in (0, 3)
]


ORDER = (
    ("across", 0),
    ("across", 1),
    ("outward", 0),
    ("across", 2),
    ("outward", 1),
    ("across", 3),
    ("gram", 0),
    ("outward", 2),
    ("sum", 1),
    ("gram_total", 0),
    ("factor", 0),
    ("outward", 3),
    ("factor", 2),
    ("factor", 3),
    ("shared", 0),
    ("shared", 2),
    ("shared", 3),
)


def fast_body(expression, usage_init, shared_factor, dataset_factors, cell_dataset, dataset_sizes):
    count, rank, genes = dataset_factors.shape
    cells = expression.shape[1]
    half = cells // 2
    tile = GENE_TILE
    core = lax.axis_index("gene") % 2
    index = core.astype(jnp.int32).reshape(1)
    place = lax.axis_index("gene").astype(jnp.int32).reshape(1)
    label = cell_dataset.reshape(1, cells)
    rows = count * rank
    flat = rank * rank // tile

    hbm = pl.BlockSpec(memory_space=pltpu.HBM)
    cell_tile = 512
    shape = (rank + count * rank * rank // half, half)
    send, keep = call(
        start_kernel,
        (index,),
        (shared_factor, dataset_factors, expression, label),
        [hbm, hbm, hbm, whole((1, cells))],
        [struct(*shape), struct(*shape)],
        [whole(shape), whole(shape)],
        scratch=[
            pltpu.VMEM((rank, genes), f32),
            pltpu.VMEM((count, rank, genes), f32),
            pltpu.VMEM((cells // cell_tile, genes, cell_tile), bf16),
            pltpu.VMEM((rows + rank, genes), bf16),
            pltpu.SemaphoreType.DMA((1 + count + cells // cell_tile,)),
        ],
        vmem=53.5,
        cost=cost(2 * (count + 1) * rank * genes * cells, 2 * genes * cells),
    )
    both = keep + swap(send, "gene", 1, 4)
    both_more = swap(both, "gene", 2, 4)
    usage_half = call(
        usage_kernel,
        (index,),
        (both, both_more, usage_init, label),
        [
            whole(shape),
            whole(shape),
            pl.BlockSpec((rank, half), lambda i, idx: (0, idx[0])),
            pl.BlockSpec((1, half), lambda i, idx: (0, idx[0])),
        ],
        struct(rank, half),
        whole((rank, half)),
        cost=cost(2 * ITERS * 3 * count * rank * rank * half, 16 * rank * half),
    )
    usage_other = swap(usage_half, "gene", 1, 4)

    pieces = pl.cdiv(genes, tile)
    columns = rank // 4
    low_half, part_half, gram_half = call(
        own_half_kernel,
        (index,),
        (usage_half, label, expression),
        [
            whole((rank, half)),
            pl.BlockSpec((1, half), lambda i, idx: (0, idx[0])),
            pl.BlockSpec((tile, half), lambda i, idx: (pieces - 1, idx[0])),
        ],
        [struct(rows, half, dtype=bf16), struct(rows, tile), struct(rows, 2 * rank)],
        [whole((rows, half)), whole((rows, tile)), whole((rows, 2 * rank))],
        cost=cost(2 * rows * (tile + 2 * rank) * half, 2 * tile * half),
    )
    other_low, first = call(
        first_stat_kernel,
        (index, place),
        (usage_other, part_half, gram_half, label, expression),
        [
            whole((rank, half)),
            whole((rows, tile)),
            whole((rows, 2 * rank)),
            pl.BlockSpec((1, half), lambda i, idx, _: (0, 1 - idx[0])),
            pl.BlockSpec((tile, half), lambda i, idx, _: (pieces - 1, 1 - idx[0])),
        ],
        [struct(rows, half, dtype=bf16), struct(rows, tile)],
        [whole((rows, half)), whole((rows, tile))],
        cost=cost(2 * rows * (tile + 2 * rank) * half, 2 * tile * half),
    )
    usage, *others = call(
        stat_kernel,
        (index,),
        (usage_half, usage_other, low_half, other_low, expression, expression),
        [
            whole((rank, half)),
            whole((rank, half)),
            whole((rows, half)),
            whole((rows, half)),
            pl.BlockSpec((tile, half), lambda i, idx: (pieces - 2 - i, idx[0])),
            pl.BlockSpec((tile, half), lambda i, idx: (pieces - 2 - i, 1 - idx[0])),
        ],
        [struct(rank, cells)] + [struct(rows, tile)] * (pieces - 1),
        [whole((rank, cells))] + [whole((rows, tile))] * (pieces - 1),
        grid=(pieces - 1,),
        cost=cost(2 * rows * genes * cells, 2 * genes * cells),
    )
    own = [first] + others

    depth = lax.axis_index("cell")
    inner = (depth == 1) | (depth == 2)
    last = pieces - 1
    inward = [lax.ppermute(part, "cell", HALF_LINE) for part in own[:last]] + [None]
    across = [None] * pieces
    outward = [None] * pieces
    totals = [None] * pieces
    token = own[1]

    def after(token, *values):
        *values, token = lax.optimization_barrier((*values, token))
        return values

    new_factors = None
    new_shared = None
    gram_left = None
    grams = None
    gram_own = None

    def shared_call(block_at, width, own_total, other_total, into):
        shape = (2 * rank, width)
        block = pl.BlockSpec((rank, width), lambda i: (0, block_at))
        more = () if into is None else (into,)
        return call(
            shared_kernel,
            (),
            (own_total, other_total, *grams, shared_factor) + more,
            [whole(shape)] * 2
            + [whole((flat, tile))] * 2
            + [block]
            + [pl.BlockSpec(memory_space=pl.ANY)] * len(more),
            struct(rank, genes),
            block,
            aliases={5: 0} if more else {},
            cost=cost(2 * 3 * 3 * rank * rank * width, 6 * 4 * rank * width),
        )

    sums = [None] * pieces

    def sum_step(j, token):
        part, got1, got2, got3 = after(token, own[j], inward[j], across[j], outward[j])
        sums[j] = part + jnp.where(inner, got1 + got2, got3)
        return sums[j]

    def factor_step(first, number, token, into):
        width = number * tile
        block_at = (pieces - first - number) // number
        gene_block = pl.BlockSpec((rank, width), lambda i, idx: (0, block_at))
        set_block = pl.BlockSpec((count, rank, width), lambda i, idx: (0, 0, block_at))
        more = () if into is None else (into,)
        shape = (2 * rank + (flat if first == 0 else 0), width)
        *crosses, _ = lax.optimization_barrier((*sums[first : first + number][::-1], token))
        into, own_total = call(
            functools.partial(factor_kernel, number),
            (dataset_sizes,),
            (*crosses, gram_left, gram_own, shared_factor, dataset_factors) + more,
            [whole((rows, tile))] * number
            + [whole((rows, 3 * rank)), whole((flat, tile)), gene_block, set_block]
            + [pl.BlockSpec(memory_space=pl.ANY)] * len(more),
            [struct(count, rank, genes), struct(*shape)],
            [set_block, whole(shape)],
            aliases={5 + number: 0} if more else {},
            cost=cost(2 * 4 * 3 * rows * rank * width, 3 * 4 * rows * width),
        )
        totals[first] = (own_total, swap(own_total, "dp", 1, 2))
        return into, own_total

    def shared_step(first, number, token, into):
        own_total, other_total = after(token, *totals[first])
        return shared_call(
            (pieces - first - number) // number,
            number * tile,
            own_total[: 2 * rank],
            other_total[: 2 * rank],
            into,
        )

    for step in ORDER:
        kind, j = step
        if kind == "across":
            part, got = after(token, own[j], inward[j])
            both = part + got
            across[j] = lax.ppermute(both, ("dp", "cell"), ACROSS)
            token = both[:8, :128] if j == 2 else got
        elif kind == "outward":
            part, got = after(token, own[j], across[j])
            both, token = part + got, got
            if j == 0:
                mixed = jnp.where(inner, both, own[last])
                inward[last] = outward[0] = lax.ppermute(mixed, "cell", HALF_LINE)
            else:
                outward[j] = lax.ppermute(both, "cell", HALF_LINE)
        elif kind == "gram":
            part, got1, got2, got3 = after(token, own[0], inward[0], across[0], outward[0])
            lanes = slice(tile - SPARE, tile - SPARE + columns)
            share = part[:, lanes] + jnp.where(
                inner, got1[:, lanes] + got2[:, lanes], got3[:, lanes]
            )
            packed = rows // 8
            share = jnp.concatenate(
                [share[i * packed : (i + 1) * packed] for i in range(8)], axis=1
            )
            pair = jnp.concatenate([share, swap(share, "gene", 1, 4)], axis=0)
            pair_got = swap(pair, "gene", 2, 4)
            token = pair
        elif kind == "gram_total":
            pair, pair_got = after(token, pair, pair_got)
            gram_left, gram_own = call(
                gram_total_kernel,
                (place, dataset_sizes),
                (pair, pair_got),
                [whole((2 * packed, 8 * columns))] * 2,
                [struct(rows, 3 * rank, dtype=bf16), struct(flat, tile)],
                [whole((rows, 3 * rank)), whole((flat, tile))],
                cost=cost(1000000, 200000),
            )
            token = gram_own
        elif kind == "sum":
            token = sum_step(j, token)
        elif kind == "factor":
            number = 2 if j == 0 else 1
            for k in range(j, j + number):
                if sums[k] is None:
                    sum_step(k, token)
            new_factors, token = factor_step(j, number, token, new_factors)
            if j == 0:
                grams = [value[2 * rank :, :tile] for value in totals[0]]
        else:
            new_shared = shared_step(j, 2 if j == 0 else 1, token, new_shared)
            token = new_shared
    return usage, new_factors, new_shared


def solution(mesh):
    sizes = (mesh.shape["dp"], mesh.shape["cell"], mesh.shape["gene"])
    return jax.shard_map(
        fast_body if sizes == (2, 4, 4) else plain_body,
        mesh=mesh,
        in_specs=(
            P("gene", ("dp", "cell")),
            P(None, ("dp", "cell")),
            P(None, "gene"),
            P("dp", None, "gene"),
            P(("dp", "cell")),
            P("dp"),
        ),
        out_specs=(P(None, ("dp", "cell")), P("dp", None, "gene"), P(None, "gene")),
        check_vma=False,
    )
```
